32 devices in a mesh: dp: 4 (over x, core), fsdp: 8 (over z, y).
Axes of the slice: x: 2, y: 2, z: 4, core: 2. Of those that a mesh axis runs over, the one named last changes fastest.
Arguments:
- tokens: bfloat16 [32768, 1024], P(('dp', 'fsdp')), may hold values from -6 to 6
- segment_ids: int32 [64, 512], P(('dp', 'fsdp')), may hold values from 0 to 5, never falling along the last dimension, each value on 1 to 200 neighbouring positions
- w_query: bfloat16 [1024, 1024], P(('dp', 'fsdp')), may hold values from -0.1875 to 0.1875
- b_query: bfloat16 [1024], P(('dp', 'fsdp')), may hold values from -3 to 3
- w_key: bfloat16 [1024, 1024], P(('dp', 'fsdp')), may hold values from -0.1875 to 0.1875
- w_value: bfloat16 [1024, 1024], P(('dp', 'fsdp')), may hold values from -0.1875 to 0.1875
- b_value: bfloat16 [1024], P(('dp', 'fsdp')), may hold values from -3 to 3
- w_out: bfloat16 [1024, 1024], P(('dp', 'fsdp')), may hold values from -1.5 to 1.5
- b_out: bfloat16 [1024], P(('dp', 'fsdp')), may hold values from -2 to 2
- ln1_gain: bfloat16 [1024], P(('dp', 'fsdp')), may hold values from 0.5 to 1.5
- ln1_bias: bfloat16 [1024], P(('dp', 'fsdp')), may hold values from -2 to 2
- w_up: bfloat16 [1024, 4096], P(('dp', 'fsdp')), may hold values from -0.1875 to 0.1875
- b_up: bfloat16 [4096], P(('dp', 'fsdp')), may hold values from -3 to 3
- w_down: bfloat16 [4096, 1024], P(('dp', 'fsdp')), may hold values from -0.09375 to 0.09375
- b_down: bfloat16 [1024], P(('dp', 'fsdp')), may hold values from -2 to 2
- ln2_gain: bfloat16 [1024], P(('dp', 'fsdp')), may hold values from 0.5 to 1.5
- ln2_bias: bfloat16 [1024], P(('dp', 'fsdp')), may hold values from -2 to 2
- out_cotangent: float32 [32768, 1024], P(('dp', 'fsdp')), may hold values from -6 to 6
Outputs:
- output: bfloat16 [32768, 1024], P(('dp', 'fsdp'))
- tokens_grad: bfloat16 [32768, 1024], P(('dp', 'fsdp'))
- w_query_grad: float32 [1024, 1024], P(('dp', 'fsdp'))
- b_query_grad: float32 [1024], P(('dp', 'fsdp'))
- w_key_grad: float32 [1024, 1024], P(('dp', 'fsdp'))
- w_value_grad: float32 [1024, 1024], P(('dp', 'fsdp'))
- b_value_grad: float32 [1024], P(('dp', 'fsdp'))
- w_out_grad: float32 [1024, 1024], P(('dp', 'fsdp'))
- b_out_grad: float32 [1024], P(('dp', 'fsdp'))
- ln1_gain_grad: float32 [1024], P(('dp', 'fsdp'))
- ln1_bias_grad: float32 [1024], P(('dp', 'fsdp'))
- w_up_grad: float32 [1024, 4096], P(('dp', 'fsdp'))
- b_up_grad: float32 [4096], P(('dp', 'fsdp'))
- w_down_grad: float32 [4096, 1024], P(('dp', 'fsdp'))
- b_down_grad: float32 [1024], P(('dp', 'fsdp'))
- ln2_gain_grad: float32 [1024], P(('dp', 'fsdp'))
- ln2_bias_grad: float32 [1024], P(('dp', 'fsdp'))
The draws below stay inside these ranges and needn't reach their ends.
Inputs may be any that keep to these rules, and one draw needn't show every extreme that they name: `segment_ids`: document numbers never fall along a sequence of 512 tokens; a document holds at most 200 tokens.
All inputs are finite; a program needn't handle non-finite values.
Results may differ from the reference program's by a relative error of at most 0.014.
Values may be sent and summed in bfloat16 or wider, within the bound.
No kernel may reach another device: no remote copies, remote signals or barrier semaphores. Data moves between devices by JAX's collectives and lax.ppermute only.
A program may use at most 256 MiB of HBM per device.

```python
import math
import jax
import jax.numpy as jnp
import numpy as np
from jax import lax

D = 1024
H = 16
DH = 64
FF = 4096
SEQ_LEN = 512
DOCS = 6
MOST_DOC = 200
SEQS = 64
TOKENS = 32768


def raised(values, stream_key, source, target, shards_of, factor):
    owner, partner = [(jnp.arange(values.shape[position]) // (values.shape[position] // shards_of)).reshape([-1 if axis == position else 1 for axis in range(values.ndim)]) for position in (source, target)]
    chosen = jax.random.permutation(stream_key, shards_of)[partner]
    strong = (owner == chosen) | (owner == (partner + shards_of // 2) % shards_of)
    return jnp.where(strong, factor * values, values)


def block_levels(own_key, dims, cuts, low, high):
    loudness = 1.0
    for axis_at, shards_of in cuts:
        steps = jax.random.uniform(jax.random.fold_in(jax.random.fold_in(own_key, 6), axis_at), (shards_of,), jnp.float32, low / len(cuts), high / len(cuts))
        loudness = loudness * jnp.repeat(jnp.exp(steps), dims[axis_at] // shards_of).reshape((-1,) + (1,) * (len(dims) - 1 - axis_at))
    return loudness


def profile(amount, total, bound, slope):
    weights = [(1 << 20) // math.isqrt(grade ** slope) + 1 for grade in range(2, amount + 1)]
    surplus, counts = total - bound - (amount - 1), [1] * (amount - 1)
    while surplus > 0:
        candidates = [i for i in range(amount - 1) if counts[i] < bound]
        whole, remaining = sum([weights[i] for i in candidates]), surplus
        for i in candidates:
            addition = min(bound - counts[i], max(1, remaining * weights[i] // whole), surplus)
            counts[i] = counts[i] + addition
            surplus = surplus - addition
    return np.array([bound] + counts)


def uneven_parts(key, number_of, total, reach, skew):
    if number_of == 2:
        one = jax.random.randint(key, (), max(1, total - reach), min(reach, total - 1) + 1)
        return jnp.stack([one, total - one])
    lengths = jnp.asarray(profile(number_of, total, reach, skew), jnp.int32)
    couples = (number_of - 1) // 2
    donor, receiver = lengths[1:1 + 2 * couples:2], lengths[2:2 + 2 * couples:2]
    room = jnp.minimum(donor - 1, reach - receiver)
    shifted = jax.random.randint(jax.random.fold_in(key, 1), (couples,), 0, 1 << 20) % (room + 1)
    lengths = lengths.at[1:1 + 2 * couples:2].set(donor - shifted).at[2:2 + 2 * couples:2].set(receiver + shifted)
    return lengths[jax.random.permutation(jax.random.fold_in(key, 2), number_of)]


def gaussian(stream_key, dims, deviation, most, cuts=(), kind=jnp.bfloat16):
    loudness = block_levels(stream_key, dims, cuts, -0.22, 0.18) if cuts else 1.0
    values = jax.random.normal(stream_key, dims, jnp.float32) * deviation * loudness
    return jnp.minimum(jnp.maximum(values, -most), most).astype(kind)


def bell_draw_with(stream_key, shape, width, bound, cuts, heavy, dtype=jnp.bfloat16):
    values = width * jax.random.normal(stream_key, shape, jnp.float32)
    if cuts:
        values = values * block_levels(stream_key, shape, cuts, -0.22, 0.18)
    return jnp.clip(raised(values, jax.random.fold_in(stream_key, 3), *heavy), -bound, bound).astype(dtype)


def setup_inputs(seed: int = 0) -> dict:
    streams_of = jax.random.split(jax.random.key(seed), 19)
    return {
        "tokens": gaussian(streams_of[0], (TOKENS, D), 1.0, 6.0, ((0, 32),)),
        "segment_ids": jax.vmap(lambda own: jnp.searchsorted(jnp.cumsum(uneven_parts(own, DOCS, SEQ_LEN, MOST_DOC, 0)), jnp.arange(SEQ_LEN), side="right"))(jax.random.split(streams_of[1], SEQS)).reshape((SEQS, SEQ_LEN)).astype(jnp.int32),
        "w_query": gaussian(streams_of[2], (D, D), D ** -0.5, 0.1875, ((0, 32),)),
        "b_query": gaussian(streams_of[3], (D,), 0.5, 3.0, ((0, 32),)),
        "w_key": gaussian(streams_of[4], (D, D), D ** -0.5, 0.1875, ((0, 32),)),
        "w_value": gaussian(streams_of[5], (D, D), D ** -0.5, 0.1875, ((0, 32),)),
        "b_value": gaussian(streams_of[6], (D,), 0.5, 3.0, ((0, 32),)),
        "w_out": gaussian(streams_of[7], (D, D), (D // 64) ** -0.5, 1.5, ((0, 32),)),
        "b_out": gaussian(streams_of[8], (D,), 0.3, 2.0, ((0, 32),)),
        "ln1_gain": jnp.clip(1.0 + 0.1 * jax.random.normal(streams_of[9], (D,), jnp.float32), 0.5, 1.5).astype(jnp.bfloat16),
        "ln1_bias": gaussian(streams_of[10], (D,), 0.3, 2.0, ((0, 32),)),
        "w_up": gaussian(streams_of[11], (D, FF), D ** -0.5, 0.1875, ((0, 32),)),
        "b_up": gaussian(streams_of[12], (FF,), 0.5, 3.0, ((0, 32),)),
        "w_down": gaussian(streams_of[13], (FF, D), FF ** -0.5, 0.09375, ((0, 32),)),
        "b_down": gaussian(streams_of[14], (D,), 0.3, 2.0, ((0, 32),)),
        "ln2_gain": jnp.clip(1.0 + 0.1 * jax.random.normal(streams_of[15], (D,), jnp.float32), 0.5, 1.5).astype(jnp.bfloat16),
        "ln2_bias": gaussian(streams_of[16], (D,), 0.3, 2.0, ((0, 32),)),
        "out_cotangent": bell_draw_with(streams_of[17], (TOKENS, D), 1.0, 6.0, ((0, 32),), (0, 1, 32, 2.75), jnp.float32),
    }


@jax.custom_vjp
def low(v):
    return lax.optimization_barrier(v.astype(jnp.bfloat16)).astype(jnp.float32)

@jax.custom_vjp
def low_back(v):
    return v

def low_keep(v):
    return (low(v), None)

def low_pass(kept, grad):
    return (grad,)

def back_keep(v):
    return (v, None)

def back_low(kept, grad):
    return (low(grad),)
low.defvjp(low_keep, low_pass)
low_back.defvjp(back_keep, back_low)

def matmul(operand, other):
    return jnp.dot(operand, other, precision=lax.Precision.HIGHEST, preferred_element_type=jnp.float32)

def layer_norm(hidden, scaling, offset):
    centred = hidden - lax.optimization_barrier(jnp.mean(hidden, axis=-1, keepdims=True))
    spread = lax.optimization_barrier(jnp.mean(centred * centred, axis=-1, keepdims=True))
    return centred * lax.rsqrt(spread + 1e-12) * scaling + offset

def attend_one(pieces):
    query_rows, key_rows, value_rows, doc_ids = pieces
    scores = jnp.einsum('qhd,khd->hqk', query_rows, key_rows, precision=lax.Precision.HIGHEST) * 0.125
    same_doc = doc_ids[:, None] == doc_ids[None, :]
    scores = low_back(jnp.where(same_doc[None], scores, -1000000000.0))
    row_peak = lax.optimization_barrier(jnp.max(scores, axis=-1, keepdims=True))
    powers = jnp.exp(scores - row_peak)
    probability = powers / lax.optimization_barrier(jnp.sum(powers, axis=-1, keepdims=True))
    mixed_heads = jnp.einsum('hqk,khd->qhd', low(probability), value_rows, precision=lax.Precision.HIGHEST)
    return mixed_heads.reshape(mixed_heads.shape[0], H * DH)

def split_heads(values, seq_count):
    return values.reshape(seq_count, SEQ_LEN, H, DH)

def layer(params, inputs, doc_ids):
    w_query, b_query, w_key, w_value, b_value, w_out, b_out, ln1_gain, ln1_bias, w_up, b_up, w_down, b_down, ln2_gain, ln2_bias = params
    seq_count = doc_ids.shape[0]
    rounded = low(inputs)
    query_rows = low(low_back(matmul(rounded, w_query) + b_query))
    key_rows = low(low_back(matmul(rounded, w_key)))
    value_rows = low(low_back(matmul(rounded, w_value) + b_value))
    mixed_heads = lax.map(jax.checkpoint(attend_one), (split_heads(query_rows, seq_count), split_heads(key_rows, seq_count), split_heads(value_rows, seq_count), doc_ids))
    mixed_heads = low(low_back(mixed_heads.reshape(seq_count * SEQ_LEN, D)))
    branch = low_back(matmul(mixed_heads, w_out) + b_out)
    first_out = layer_norm(inputs + branch, ln1_gain, ln1_bias)
    upward = low_back(matmul(low(first_out), w_up) + b_up)
    active = low(jax.nn.gelu(upward, approximate=False))
    second = low_back(matmul(active, w_down) + b_down)
    return layer_norm(first_out + second, ln2_gain, ln2_bias)

def reference(tokens, segment_ids, w_query, b_query, w_key, w_value, b_value, w_out, b_out, ln1_gain, ln1_bias, w_up, b_up, w_down, b_down, ln2_gain, ln2_bias, out_cotangent):
    weights = (w_query, b_query, w_key, w_value, b_value, w_out, b_out, ln1_gain, ln1_bias, w_up, b_up, w_down, b_down, ln2_gain, ln2_bias)
    weights = tuple((item.astype(jnp.float32) for item in weights))
    group_size = math.gcd(SEQS, max(1, 4096 // SEQ_LEN))
    rounds = SEQS // group_size
    inputs = tokens.astype(jnp.float32).reshape(rounds, group_size * SEQ_LEN, D)
    doc_blocks = segment_ids.reshape(rounds, group_size, SEQ_LEN)
    tangents = out_cotangent.astype(jnp.float32).reshape(rounds, group_size * SEQ_LEN, D)

    def scan_step(totals, pieces):
        row_block, doc_ids, tangent = pieces

        def forward(params, values):
            return layer(params, values, doc_ids)
        result, pullback = jax.vjp(forward, weights, row_block)
        grad_params, grad_inputs = pullback(tangent)
        totals = jax.tree.map(jnp.add, totals, grad_params)
        return (totals, (result.astype(jnp.bfloat16), grad_inputs.astype(jnp.bfloat16)))
    starts = tuple((jnp.zeros_like(item) for item in weights))
    totals, (out_rows, grad_rows) = lax.scan(scan_step, starts, (inputs, doc_blocks, tangents))
    return (out_rows.reshape(TOKENS, D), grad_rows.reshape(TOKENS, D), totals[0], totals[1], totals[2], totals[3], totals[4], totals[5], totals[6], totals[7], totals[8], totals[9], totals[10], totals[11], totals[12], totals[13], totals[14])
```

```python
import functools

import jax
import jax.numpy as jnp
from jax import lax
from jax.experimental import pallas as pl
from jax.experimental.pallas import tpu as pltpu
from jax.sharding import PartitionSpec as P

D = 1024
H = 16
DH = 64
SEQ_LEN = 512
AXES = ("dp", "fsdp")
CORES = 2


def matmul(operand, other):
    return jnp.dot(operand, other, preferred_element_type=jnp.float32)


def back_matmul(operand, other):
    return lax.dot_general(
        operand, other, (((1,), (1,)), ((), ())), preferred_element_type=jnp.float32
    )


def outer_sum(operand, other):
    return lax.dot_general(
        operand, other, (((0,), (0,)), ((), ())), preferred_element_type=jnp.float32
    )


def column_sum(values):
    return jnp.sum(values.astype(jnp.float32), axis=0)


def norm_forward(hidden):
    centred = hidden - jnp.mean(hidden, axis=-1, keepdims=True)
    scale_row = lax.rsqrt(jnp.mean(centred * centred, axis=-1, keepdims=True) + 1e-12)
    return (centred * scale_row, scale_row)


def norm_backward(grad_out, normed, scale_row, scaling):
    scaled = grad_out * scaling
    return scale_row * (
        scaled
        - jnp.mean(scaled, axis=-1, keepdims=True)
        - normed * jnp.mean(scaled * normed, axis=-1, keepdims=True)
    )


def gelu_slope(values):
    return (
        0.5 * (1.0 + lax.erf(values * 0.7071067811865476))
        + values * jnp.exp(-0.5 * values * values) * 0.3989422804014327
    )


def masked_scores(query_rows, key_rows, doc_ids):
    scores = (
        jnp.einsum("qhd,khd->hqk", query_rows, key_rows, preferred_element_type=jnp.float32) * 0.125
    )
    same_doc = doc_ids[:, None] == doc_ids[None, :]
    return jnp.where(same_doc[None], scores, -1000000000.0)


def attend_forward(pieces):
    query_rows, key_rows, value_rows, doc_ids = pieces
    scores = masked_scores(query_rows, key_rows, doc_ids)
    row_peak = jnp.max(scores, axis=-1, keepdims=True)
    powers = jnp.exp(scores - row_peak)
    row_total = jnp.sum(powers, axis=-1, keepdims=True)
    probability = (powers / row_total).astype(jnp.bfloat16)
    mixed_heads = jnp.einsum(
        "hqk,khd->qhd", probability, value_rows, preferred_element_type=jnp.float32
    )
    logsum = (row_peak + jnp.log(row_total))[:, :, 0]
    return (mixed_heads.astype(jnp.bfloat16).reshape(mixed_heads.shape[0], H * DH), logsum)


def attend_backward(pieces):
    query_rows, key_rows, value_rows, doc_ids, logsum, grad_heads = pieces
    scores = masked_scores(query_rows, key_rows, doc_ids)
    probability = jnp.exp(scores - logsum[:, :, None])
    grad_prob = jnp.einsum(
        "qhd,khd->hqk", grad_heads, value_rows, preferred_element_type=jnp.float32
    )
    row_delta = jnp.sum(probability * grad_prob, axis=-1, keepdims=True)
    grad_scores = (probability * (grad_prob - row_delta)).astype(jnp.bfloat16)
    grad_query = (
        jnp.einsum("hqk,khd->qhd", grad_scores, key_rows, preferred_element_type=jnp.float32)
        * 0.125
    )
    grad_key = (
        jnp.einsum("hqk,qhd->khd", grad_scores, query_rows, preferred_element_type=jnp.float32)
        * 0.125
    )
    grad_value = jnp.einsum(
        "hqk,qhd->khd",
        probability.astype(jnp.bfloat16),
        grad_heads,
        preferred_element_type=jnp.float32,
    )
    return (
        grad_query.astype(jnp.bfloat16),
        grad_key.astype(jnp.bfloat16),
        grad_value.astype(jnp.bfloat16),
    )


class Grid:
    def __init__(self, mesh):
        self.shape = dict(mesh.shape)
        self.xs = self.shape["dp"] // CORES
        self.ys = self.xs
        self.zs = self.shape["fsdp"] // self.ys
        self.sizes = {"x": self.xs, "c": CORES, "z": self.zs, "y": self.ys}
        self.count = self.shape["dp"] * self.shape["fsdp"]
        self.pairs = self.xs == 2 and self.ys == 2

    def at(self):
        dp, fsdp = lax.axis_index("dp"), lax.axis_index("fsdp")
        return {"x": dp // CORES, "c": dp % CORES, "z": fsdp // self.ys, "y": fsdp % self.ys}

    def shifted(self, axis, step, wrap):
        hops = []
        for x in range(self.xs):
            for c in range(CORES):
                for z in range(self.zs):
                    for y in range(self.ys):
                        to = {"x": x, "c": c, "z": z, "y": y}
                        to[axis] += step
                        if wrap:
                            to[axis] %= self.sizes[axis]
                        elif not 0 <= to[axis] < self.sizes[axis]:
                            continue
                        hops.append((self.number(x, c, z, y), self.number(**to)))
        return hops

    def number(self, x, c, z, y):
        return ((x * CORES + c) * self.zs + z) * self.ys + y

    def swap(self, values, axis):
        return lax.ppermute(values, AXES, self.shifted(axis, 1, True))

    def along(self, values, axis, step):
        return lax.ppermute(values, AXES, self.shifted(axis, step, False))


def line_gather(grid, at, shard):
    up, down = [shard], [shard]
    for _ in range(grid.zs - 1):
        up.append(grid.along(up[-1], "z", 1))
        down.append(grid.along(down[-1], "z", -1))
    line = jnp.stack(up[:0:-1] + [shard] + down[1:])
    return lax.dynamic_slice_in_dim(line, grid.zs - 1 - at["z"], grid.zs, 0)


def pair_gather(grid, block, first, second):
    near = grid.swap(block, first)
    pieces = {(0, 0): block, (1, 0): near}
    pieces[(0, 1)] = grid.swap(block, second)
    pieces[(1, 1)] = grid.swap(near, second)
    found = {}
    for (one, two), piece in pieces.items():
        flips = {first: one, second: two}
        found[(flips["x"], 0, flips["y"])] = piece
        found[(flips["x"], 1, flips["y"])] = grid.swap(piece, "c")
    return found


def assemble_kernel(plan, grid, count, outs, spot, *refs):
    pieces, whole, sem = refs[:count], refs[count : count + outs], refs[-1]
    copies = []
    for source, (flip, out, rows, columns, start) in enumerate_plan(plan):
        x, c, y = ((spot[i] + flip[i]) % 2 for i in range(3))
        copies.append(
            pltpu.make_async_copy(
                pieces[source].at[:, pl.ds(start, rows), :],
                whole[out].at[x, c, :, y, :, pl.ds(columns[0], columns[1])],
                sem.at[len(copies)],
            )
        )
    for copy in copies:
        copy.start()
    for copy in copies:
        copy.wait()


def enumerate_plan(plan):
    for source, (flip, targets) in enumerate(plan):
        for out, rows, columns, start in targets:
            yield source, (flip, out, rows, columns, start)


def assemble(grid, at, parts, shapes):
    plan, arrays = [], []
    for pieces, targets in parts:
        for flip, piece in pieces.items():
            plan.append((flip, targets))
            arrays.append(piece)
    copies = sum(len(targets) for _, targets in plan)
    spot = jnp.stack([at["x"], at["c"], at["y"]]).astype(jnp.int32)
    outs = [
        jax.ShapeDtypeStruct((grid.xs, CORES, grid.zs, grid.ys) + shape, jnp.bfloat16)
        for shape in shapes
    ]
    size = sum(2 * piece.size for piece in arrays)
    whole = pl.pallas_call(
        functools.partial(assemble_kernel, plan, grid, len(arrays), len(outs)),
        out_shape=outs,
        in_specs=[pl.BlockSpec(memory_space=pltpu.SMEM)]
        + [pl.BlockSpec(memory_space=pl.ANY)] * len(arrays),
        out_specs=[pl.BlockSpec(memory_space=pl.ANY)] * len(outs),
        scratch_shapes=[pltpu.SemaphoreType.DMA((copies,))],
        cost_estimate=pl.CostEstimate(flops=0, bytes_accessed=2 * size, transcendentals=0),
        compiler_params=pltpu.CompilerParams(vmem_limit_bytes=1 << 20),
    )(spot, *arrays)
    return [w.reshape(grid.count * s[0], s[1]) for w, s in zip(whole, shapes)]


def take(values, index, axis):
    return lax.dynamic_index_in_dim(values, index, axis, keepdims=False)


def total(terms):
    result = terms[0].astype(jnp.float32)
    for term in terms[1:]:
        result = result + term.astype(jnp.float32)
    return result


def swap_reduce(grid, at, terms, name, axis):
    sent = total([take(term, 1 - at[name], axis) for term in terms]).astype(terms[0].dtype)
    got = grid.swap(sent, name)
    return [take(term, at[name], axis) for term in terms] + [got]


def line_reduce(grid, at, terms):
    size, kind = grid.zs, terms[0].dtype

    def own(index):
        index = jnp.clip(index, 0, size - 1)
        return total([take(term, index, 0) for term in terms])

    up = down = None
    for step in range(1, size):
        up_sum, down_sum = own(at["z"] + size - step), own(at["z"] - size + step)
        if step > 1:
            up_sum, down_sum = up_sum + up.astype(jnp.float32), down_sum + down.astype(jnp.float32)
        up = grid.along(up_sum.astype(kind), "z", 1)
        down = grid.along(down_sum.astype(kind), "z", -1)
    return own(at["z"]) + up.astype(jnp.float32) + down.astype(jnp.float32)


def chip_reduce(grid, at, terms, order):
    if order == "xy":
        terms = swap_reduce(grid, at, terms, "x", 0)
        terms = swap_reduce(grid, at, terms, "y", 1)
    else:
        terms = swap_reduce(grid, at, terms, "y", 2)
        terms = swap_reduce(grid, at, terms, "x", 0)
    return line_reduce(grid, at, terms)


def product_reduce(grid, at, left, right, cuts):
    rows = left.shape[1] // grid.count
    split = left.reshape(left.shape[0], grid.xs, CORES, -1)

    def half(core):
        part = take(split, core, 2).reshape(left.shape[0], -1)
        return outer_sum(part, right).astype(jnp.bfloat16)

    sent, kept = half(1 - at["c"]), half(at["c"])
    got = grid.swap(sent, "c")
    shape = (grid.xs, grid.zs, grid.ys, rows)
    results, start = [], 0
    for width, order in cuts:
        terms = [
            part[:, start : start + width].reshape(shape + (width,)) for part in (kept, got)
        ]
        results.append(chip_reduce(grid, at, terms, order))
        start += width
    return jnp.concatenate(results, axis=1) if len(results) > 1 else results[0]


def small_reduce(grid, at, vectors):
    packed = jnp.concatenate([v.reshape(grid.count, -1) for v in vectors], axis=1)
    width = packed.shape[1]
    lines = -(-width // 128)
    packed = jnp.pad(packed, ((0, 0), (0, lines * 128 - width)))
    packed = packed.reshape(grid.xs, CORES, grid.zs, grid.ys, lines, 128)
    terms = swap_reduce(grid, at, [packed], "c", 1)
    flat = chip_reduce(grid, at, terms, "xy").reshape(-1)
    results, start = [], 0
    for vector in vectors:
        size = vector.size // grid.count
        results.append(flat[start : start + size])
        start += size
    return results


def gather_weights(grid, at, attn, smalls, w_out, w_up, w_down):
    rows = attn[0].shape[0]
    widths = [small.shape[0] for small in smalls]
    if not grid.pairs:
        whole = [lax.all_gather(w, AXES, axis=0, tiled=True) for w in (*attn, w_out, w_up, w_down)]
        small = lax.all_gather(jnp.concatenate(smalls), AXES, axis=0, tiled=True)
        small = small.reshape(grid.count, -1)
        return jnp.concatenate(whole[:3], axis=1), split_small(small, widths), *whole[3:]
    packed = jnp.pad(jnp.concatenate(smalls), (0, rows * 128 - sum(widths))).reshape(rows, 128)
    first = line_gather(grid, at, jnp.concatenate([*attn, packed], axis=1))
    columns = first.shape[2]
    cut = (columns // 256) * 128
    left = pair_gather(grid, first[:, :, :cut], "y", "x")
    right = pair_gather(grid, first[:, :, cut:], "x", "y")
    (wide,) = assemble(
        grid,
        at,
        [(left, [(0, rows, (0, cut), 0)]), (right, [(0, rows, (cut, columns - cut), 0)])],
        [(rows, columns)],
    )
    small = wide[:, 3 * D :].reshape(grid.count, -1)
    second = line_gather(grid, at, jnp.concatenate([w_out, w_down], axis=0))
    third = line_gather(grid, at, w_up)
    second = pair_gather(grid, second, "y", "x")
    third = pair_gather(grid, third, "x", "y")
    lower = w_down.shape[0]
    (full_up,) = assemble(
        grid, at, [(third, [(0, rows, (0, w_up.shape[1]), 0)])], [(rows, w_up.shape[1])]
    )
    full_out, full_down = assemble(
        grid,
        at,
        [(second, [(0, rows, (0, D), 0), (1, lower, (0, D), rows)])],
        [(rows, D), (lower, D)],
    )
    return wide[:, : 3 * D], split_small(small, widths), full_out, full_up, full_down


def split_small(small, widths):
    results, start = [], 0
    for width in widths:
        results.append(small[:, start : start + width].reshape(-1).astype(jnp.float32))
        start += width
    return results


def reduce_product(grid, at, left, right, cuts):
    if grid.pairs:
        return product_reduce(grid, at, left, right, cuts)
    return lax.psum_scatter(outer_sum(left, right), AXES, scatter_dimension=0, tiled=True)


def per_device(
    grid,
    tokens,
    segment_ids,
    w_query,
    b_query,
    w_key,
    w_value,
    b_value,
    w_out,
    b_out,
    ln1_gain,
    ln1_bias,
    w_up,
    b_up,
    w_down,
    b_down,
    ln2_gain,
    ln2_bias,
    out_cotangent,
):
    at = grid.at()
    full_qkv, smalls, full_out, full_up, full_down = gather_weights(
        grid,
        at,
        (w_query, w_key, w_value),
        (b_query, b_value, b_out, ln1_gain, ln1_bias, b_up, b_down, ln2_gain, ln2_bias),
        w_out,
        w_up,
        w_down,
    )
    bias_query, bias_value, bias_out, gain_one, shift_one = smalls[:5]
    bias_up, bias_down, gain_two, shift_two = smalls[5:]
    seq_count = segment_ids.shape[0]
    row_count = tokens.shape[0]
    head_shape = (seq_count, SEQ_LEN, H, DH)
    inputs = tokens.astype(jnp.float32)
    bias_qkv = jnp.concatenate([bias_query, jnp.zeros_like(bias_query), bias_value])
    qkv = (matmul(tokens, full_qkv) + bias_qkv).astype(jnp.bfloat16)
    query_rows, key_rows, value_rows = (
        qkv[:, i * D : (i + 1) * D].reshape(head_shape) for i in range(3)
    )
    mixed_heads, logsum = lax.map(attend_forward, (query_rows, key_rows, value_rows, segment_ids))
    mixed_heads = mixed_heads.reshape(row_count, H * DH)
    hidden = inputs + matmul(mixed_heads, full_out) + bias_out
    normed_one, scale_one = norm_forward(hidden)
    first_out = normed_one * gain_one + shift_one
    first_low = first_out.astype(jnp.bfloat16)
    upward = matmul(first_low, full_up) + bias_up
    active = jax.nn.gelu(upward, approximate=False).astype(jnp.bfloat16)
    second = matmul(active, full_down) + bias_down
    normed_two, scale_two = norm_forward(first_out + second)
    output = (normed_two * gain_two + shift_two).astype(jnp.bfloat16)
    grad_gain_two = jnp.sum(out_cotangent * normed_two, axis=0)
    grad_shift_two = jnp.sum(out_cotangent, axis=0)
    grad_sum_two = norm_backward(out_cotangent, normed_two, scale_two, gain_two)
    grad_second = grad_sum_two.astype(jnp.bfloat16)
    share_down = reduce_product(grid, at, active, grad_second, [(D, "xy")])
    grad_bias_down = column_sum(grad_second)
    grad_upward = (back_matmul(grad_second, full_down) * gelu_slope(upward)).astype(jnp.bfloat16)
    share_up = reduce_product(grid, at, first_low, grad_upward, [(grad_upward.shape[1], "yx")])
    grad_bias_up = column_sum(grad_upward)
    grad_first = grad_sum_two + back_matmul(grad_upward, full_up)
    grad_gain_one = jnp.sum(grad_first * normed_one, axis=0)
    grad_shift_one = jnp.sum(grad_first, axis=0)
    grad_hidden = norm_backward(grad_first, normed_one, scale_one, gain_one)
    grad_branch = grad_hidden.astype(jnp.bfloat16)
    share_out = reduce_product(grid, at, mixed_heads, grad_branch, [(D, "xy")])
    grad_bias_out = column_sum(grad_branch)
    grad_mixed = back_matmul(grad_branch, full_out).astype(jnp.bfloat16).reshape(head_shape)
    grads = lax.map(
        attend_backward, (query_rows, key_rows, value_rows, segment_ids, logsum, grad_mixed)
    )
    grad_qkv = jnp.concatenate([grad.reshape(row_count, D) for grad in grads], axis=1)
    share_qkv = reduce_product(grid, at, tokens, grad_qkv, [(D * 3 // 2, "xy"), (D * 3 // 2, "yx")])
    tokens_grad = (grad_hidden + back_matmul(grad_qkv, full_qkv)).astype(jnp.bfloat16)
    grad_bias_qkv = column_sum(grad_qkv)
    vectors = [
        grad_bias_qkv[:D],
        grad_bias_qkv[2 * D :],
        grad_bias_out,
        grad_gain_one,
        grad_shift_one,
        grad_bias_up,
        grad_bias_down,
        grad_gain_two,
        grad_shift_two,
    ]
    if grid.pairs:
        shares = small_reduce(grid, at, vectors)
    else:
        shares = [lax.psum_scatter(v, AXES, scatter_dimension=0, tiled=True) for v in vectors]
    return (
        output,
        tokens_grad,
        share_qkv[:, :D],
        shares[0],
        share_qkv[:, D : 2 * D],
        share_qkv[:, 2 * D :],
        shares[1],
        share_out,
        *shares[2:5],
        share_up,
        shares[5],
        share_down,
        *shares[6:],
    )


def solution(mesh):
    rows, flat = P(AXES, None), P(AXES)
    in_specs = (rows,) * 3 + (flat, rows, rows, flat, rows, flat, flat, flat, rows, flat, rows)
    in_specs += (flat,) * 3 + (rows,)
    out_specs = (rows,) * 3 + (flat, rows, rows, flat, rows, flat, flat, flat, rows, flat, rows)
    out_specs += (flat,) * 3
    return jax.shard_map(
        functools.partial(per_device, Grid(mesh)),
        mesh=mesh,
        in_specs=in_specs,
        out_specs=out_specs,
        check_vma=False,
    )
```

```python
import functools

import jax
import jax.numpy as jnp
from jax import lax
from jax.experimental import pallas as pl
from jax.experimental.pallas import tpu as pltpu
from jax.sharding import PartitionSpec as P

D = 1024
H = 16
DH = 64
SEQ_LEN = 512
AXES = ("dp", "fsdp")
CORES = 2


def matmul(operand, other):
    return jnp.dot(operand, other, preferred_element_type=jnp.float32)


def back_matmul(operand, other):
    return lax.dot_general(
        operand, other, (((1,), (1,)), ((), ())), preferred_element_type=jnp.float32
    )


def outer_sum(operand, other):
    return lax.dot_general(
        operand, other, (((0,), (0,)), ((), ())), preferred_element_type=jnp.float32
    )


def column_sum(values):
    return jnp.sum(values.astype(jnp.float32), axis=0)


def norm_forward(hidden):
    centred = hidden - jnp.mean(hidden, axis=-1, keepdims=True)
    scale_row = lax.rsqrt(jnp.mean(centred * centred, axis=-1, keepdims=True) + 1e-12)
    return (centred * scale_row, scale_row)


def norm_backward(grad_out, normed, scale_row, scaling):
    scaled = grad_out * scaling
    return scale_row * (
        scaled
        - jnp.mean(scaled, axis=-1, keepdims=True)
        - normed * jnp.mean(scaled * normed, axis=-1, keepdims=True)
    )


def across(operand, other):
    return lax.dot_general(
        operand, other, (((1,), (1,)), ((), ())), preferred_element_type=jnp.float32
    )


def down(operand, other):
    return lax.dot_general(
        operand, other, (((0,), (0,)), ((), ())), preferred_element_type=jnp.float32
    )


def attend_forward_kernel(query, key, value, doc_column, doc_row, mixed):
    same = doc_column[0] == doc_row[0]
    heads = []
    for head in range(2):
        lanes = slice(head * DH, (head + 1) * DH)
        scores = across(key[:, lanes], query[:, lanes] * jnp.bfloat16(0.125))
        scores = jnp.where(same, scores, -1000000000.0)
        powers = jnp.exp(scores - jnp.max(scores, axis=0, keepdims=True))
        row_total = jnp.sum(powers, axis=0, keepdims=True)
        heads.append(down(value[:, lanes], powers.astype(jnp.bfloat16)) * (1.0 / row_total))
    mixed[...] = jnp.concatenate(heads, axis=0).T.astype(jnp.bfloat16)


def attend_backward_kernel(query, key, value, grad, doc_column, doc_row, out, sums):
    same = doc_column[0] == doc_row[0]
    step = pl.program_id(1)
    found = ([], [], [])
    for head in range(2):
        lanes = slice(head * DH, (head + 1) * DH)
        scaled = query[:, lanes] * jnp.bfloat16(0.125)
        scores = jnp.where(same, across(key[:, lanes], scaled), -1000000000.0)
        powers = jnp.exp(scores - jnp.max(scores, axis=0, keepdims=True))
        probability = powers * (1.0 / jnp.sum(powers, axis=0, keepdims=True))
        grad_prob = across(value[:, lanes], grad[:, lanes])
        delta = jnp.sum(probability * grad_prob, axis=0, keepdims=True)
        grad_scores = (probability * (grad_prob - delta)).astype(jnp.bfloat16)
        found[0].append(down(key[:, lanes], grad_scores) * 0.125)
        found[1].append(matmul(grad_scores, scaled))
        found[2].append(matmul(probability.astype(jnp.bfloat16), grad[:, lanes]))
    grads = (
        jnp.concatenate(found[0], axis=0).T,
        jnp.concatenate(found[1], axis=1),
        jnp.concatenate(found[2], axis=1),
    )
    first = pl.program_id(0) == 0
    for index, value_of in enumerate(grads):
        rounded = value_of.astype(jnp.bfloat16)
        place = pl.ds(pl.multiple_of(index * HALF + step * 128, 128), 128)
        out[:, place] = rounded
        if index != 1:
            more = jnp.sum(rounded.astype(jnp.float32), axis=0, keepdims=True)
            sums[:, place] = jnp.where(first, 0.0, sums[:, place]) + more


HALF = D // 2
PAIRS = HALF // 128


def head_specs(start):
    def block(part):
        def index(seq, pair):
            pair = pair + start
            return seq, pair // PAIRS * (3 * PAIRS) + part * PAIRS + pair % PAIRS

        return pl.BlockSpec((SEQ_LEN, 128), index)

    docs = [
        pl.BlockSpec((1, SEQ_LEN, 1), lambda seq, pair: (seq, 0, 0)),
        pl.BlockSpec((1, 1, SEQ_LEN), lambda seq, pair: (seq, 0, 0)),
    ]
    return [block(i) for i in range(3)], docs


def attend_forward(qkv, doc_column, doc_row):
    seqs = doc_row.shape[0]
    heads, docs = head_specs(0)
    work = seqs * H * SEQ_LEN * SEQ_LEN
    return pl.pallas_call(
        attend_forward_kernel,
        grid=(seqs, 2 * PAIRS),
        out_shape=jax.ShapeDtypeStruct((seqs * SEQ_LEN, D), jnp.bfloat16),
        in_specs=heads + docs,
        out_specs=pl.BlockSpec((SEQ_LEN, 128), lambda seq, pair: (seq, pair)),
        cost_estimate=pl.CostEstimate(
            flops=16 * DH * work, bytes_accessed=8 * qkv.size, transcendentals=work
        ),
        compiler_params=pltpu.CompilerParams(vmem_limit_bytes=40 << 20),
    )(qkv, qkv, qkv, doc_column, doc_row)


def attend_backward(qkv, grad_mixed, doc_column, doc_row, half):
    seqs = doc_row.shape[0]
    heads, docs = head_specs(half * PAIRS)
    work = seqs * H * SEQ_LEN * SEQ_LEN // 2
    return pl.pallas_call(
        attend_backward_kernel,
        grid=(seqs, PAIRS),
        out_shape=[
            jax.ShapeDtypeStruct((seqs * SEQ_LEN, 3 * HALF), jnp.bfloat16),
            jax.ShapeDtypeStruct((1, 3 * HALF), jnp.float32),
        ],
        in_specs=heads
        + [pl.BlockSpec((SEQ_LEN, 128), lambda seq, pair: (seq, half * PAIRS + pair))]
        + docs,
        out_specs=[
            pl.BlockSpec((SEQ_LEN, 3 * HALF), lambda seq, pair: (seq, 0)),
            pl.BlockSpec((1, 3 * HALF), lambda seq, pair: (0, 0)),
        ],
        cost_estimate=pl.CostEstimate(
            flops=40 * DH * work, bytes_accessed=8 * qkv.size, transcendentals=work
        ),
        compiler_params=pltpu.CompilerParams(vmem_limit_bytes=50 << 20),
    )(qkv, qkv, qkv, grad_mixed, doc_column, doc_row)


CHUNK = 512
TILE = 256


def part_out(spot, values, parted, blocks):
    width = values.shape[1] // blocks
    for block in range(blocks):
        half = (block % 2 + spot[0] + 1) % 2
        start = block // 2 * width
        parted[half, :, start : start + width] = values[:, block * width : (block + 1) * width]


def middle_forward_kernel(
    blocks,
    spot,
    mixed,
    tokens,
    cotangent,
    w_out,
    w_up,
    w_down,
    vectors,
    bias_up,
    output,
    grad_sum,
    grad_low,
    normed,
    scale,
    active_parts,
    slope,
    first_parts,
    mixed_parts,
    token_parts,
    sums,
):
    bias_out, gain_one, shift_one, bias_down, gain_two, shift_two = (
        vectors[i : i + 1, :] for i in range(6)
    )
    part_out(spot, mixed[...], mixed_parts, blocks)
    part_out(spot, tokens[...], token_parts, blocks)
    hidden = tokens[...].astype(jnp.float32) + matmul(mixed[...], w_out[...]) + bias_out
    normed_one, scale_one = norm_forward(hidden)
    normed[...] = normed_one
    scale[...] = jnp.broadcast_to(scale_one, scale.shape)
    first_out = normed_one * gain_one + shift_one
    first_low = first_out.astype(jnp.bfloat16)
    part_out(spot, first_low, first_parts, blocks)
    width = w_up.shape[1] // blocks
    second = first_out + bias_down
    for start in range(0, w_up.shape[1], CHUNK):
        at = slice(start, start + CHUNK)
        upward = matmul(first_low, w_up[:, at]) + bias_up[:, at]
        phi = 0.5 * (1.0 + lax.erf(upward * 0.7071067811865476))
        active = (upward * phi).astype(jnp.bfloat16)
        slope[:, at] = (
            phi + upward * jnp.exp(-0.5 * upward * upward) * 0.3989422804014327
        ).astype(jnp.bfloat16)
        block, inside = start // width, start % width
        half = (block % 2 + spot[0] + 1) % 2
        place = block // 2 * width + inside
        active_parts[half, :, place : place + CHUNK] = active
        second = second + matmul(active, w_down[at, :])
    normed_two, scale_two = norm_forward(second)
    output[...] = (normed_two * gain_two + shift_two).astype(jnp.bfloat16)
    grad = cotangent[...]
    grad_second = norm_backward(grad, normed_two, scale_two, gain_two)
    grad_sum[...] = grad_second
    rounded = grad_second.astype(jnp.bfloat16)
    grad_low[...] = rounded

    @pl.when(pl.program_id(0) == 0)
    def _():
        sums[...] = jnp.zeros_like(sums)

    sums[0:1, :] += jnp.sum(grad * normed_two, axis=0, keepdims=True)
    sums[1:2, :] += jnp.sum(grad, axis=0, keepdims=True)
    sums[2:3, :] += jnp.sum(rounded.astype(jnp.float32), axis=0, keepdims=True)


def middle_backward_kernel(
    grad_low,
    grad_sum,
    slope,
    normed,
    scale,
    w_out,
    w_up,
    w_down,
    vectors,
    grad_up,
    grad_hidden,
    branch,
    grad_mixed,
    sums,
    sums_up,
):
    @pl.when(pl.program_id(0) == 0)
    def _():
        sums[...] = jnp.zeros_like(sums)
        sums_up[...] = jnp.zeros_like(sums_up)

    grad_first = grad_sum[...]
    low = grad_low[...]
    for start in range(0, w_up.shape[1], CHUNK):
        at = slice(start, start + CHUNK)
        part = (across(low, w_down[at, :]) * slope[:, at].astype(jnp.float32)).astype(jnp.bfloat16)
        grad_up[:, at] = part
        sums_up[:, at] += jnp.sum(part.astype(jnp.float32), axis=0, keepdims=True)
        grad_first = grad_first + across(part, w_up[:, at])
    normed_one = normed[...]
    sums[0:1, :] += jnp.sum(grad_first * normed_one, axis=0, keepdims=True)
    sums[1:2, :] += jnp.sum(grad_first, axis=0, keepdims=True)
    hidden = norm_backward(grad_first, normed_one, scale[:, 0:1], vectors[1:2, :])
    grad_hidden[...] = hidden
    rounded = hidden.astype(jnp.bfloat16)
    branch[...] = rounded
    sums[2:3, :] += jnp.sum(rounded.astype(jnp.float32), axis=0, keepdims=True)
    grad_mixed[...] = across(rounded, w_out[...]).astype(jnp.bfloat16)


def tiled(columns):
    return pl.BlockSpec((TILE, columns), lambda i: (i, 0))


def parted(columns):
    return pl.BlockSpec((2, TILE, columns), lambda i: (0, i, 0))


def resident(shape):
    return pl.BlockSpec(shape, lambda i: (0,) * len(shape), pipeline_mode=pl.Buffered(1))


def middle_forward(core, blocks, mixed, tokens, cotangent, w_out, w_up, w_down, vectors, bias_up):
    rows, wide = tokens.shape[0], w_up.shape[1]
    shapes = [
        ((rows, D), jnp.bfloat16),
        ((rows, D), jnp.float32),
        ((rows, D), jnp.bfloat16),
        ((rows, D), jnp.float32),
        ((rows, 128), jnp.float32),
        ((2, rows, wide // 2), jnp.bfloat16),
        ((rows, wide), jnp.bfloat16),
        ((2, rows, D // 2), jnp.bfloat16),
        ((2, rows, D // 2), jnp.bfloat16),
        ((2, rows, D // 2), jnp.bfloat16),
        ((8, D), jnp.float32),
    ]
    specs = [parted(s[2]) if len(s) == 3 else tiled(s[1]) for s, _ in shapes[:-1]]
    return pl.pallas_call(
        functools.partial(middle_forward_kernel, blocks),
        grid=(rows // TILE,),
        out_shape=[jax.ShapeDtypeStruct(*s) for s in shapes],
        in_specs=[pl.BlockSpec(memory_space=pltpu.SMEM)]
        + [tiled(D)] * 3
        + [resident(w.shape) for w in (w_out, w_up, w_down, vectors, bias_up)],
        out_specs=specs + [pl.BlockSpec((8, D), lambda i: (0, 0))],
        cost_estimate=pl.CostEstimate(
            flops=2 * rows * (D * D + 2 * D * wide),
            bytes_accessed=60 << 20,
            transcendentals=2 * rows * wide,
        ),
        compiler_params=pltpu.CompilerParams(vmem_limit_bytes=60 << 20),
    )(core, mixed, tokens, cotangent, w_out, w_up, w_down, vectors, bias_up)


def middle_backward(grad_low, grad_sum, slope, normed, scale, w_out, w_up, w_down, vectors):
    rows, wide = grad_low.shape[0], w_up.shape[1]
    shapes = [
        ((rows, wide), jnp.bfloat16),
        ((rows, D), jnp.float32),
        ((rows, D), jnp.bfloat16),
        ((rows, D), jnp.bfloat16),
    ]
    last = [((8, D), jnp.float32), ((1, wide), jnp.float32)]
    return pl.pallas_call(
        middle_backward_kernel,
        grid=(rows // TILE,),
        out_shape=[jax.ShapeDtypeStruct(*s) for s in shapes + last],
        in_specs=[tiled(v.shape[1]) for v in (grad_low, grad_sum, slope, normed, scale)]
        + [resident(w.shape) for w in (w_out, w_up, w_down, vectors)],
        out_specs=[tiled(s[1]) for s, _ in shapes]
        + [pl.BlockSpec(s, lambda i: (0, 0)) for s, _ in last],
        cost_estimate=pl.CostEstimate(
            flops=2 * rows * (D * D + 2 * D * wide), bytes_accessed=60 << 20, transcendentals=0
        ),
        compiler_params=pltpu.CompilerParams(vmem_limit_bytes=60 << 20),
    )(grad_low, grad_sum, slope, normed, scale, w_out, w_up, w_down, vectors)


class Grid:
    def __init__(self, mesh):
        self.shape = dict(mesh.shape)
        self.xs = self.shape["dp"] // CORES
        self.ys = self.xs
        self.zs = self.shape["fsdp"] // self.ys
        self.sizes = {"x": self.xs, "c": CORES, "z": self.zs, "y": self.ys}
        self.count = self.shape["dp"] * self.shape["fsdp"]
        self.pairs = self.xs == 2 and self.ys == 2

    def at(self):
        dp, fsdp = lax.axis_index("dp"), lax.axis_index("fsdp")
        return {"x": dp // CORES, "c": dp % CORES, "z": fsdp // self.ys, "y": fsdp % self.ys}

    def shifted(self, axis, step, wrap):
        hops = []
        for x in range(self.xs):
            for c in range(CORES):
                for z in range(self.zs):
                    for y in range(self.ys):
                        to = {"x": x, "c": c, "z": z, "y": y}
                        to[axis] += step
                        if wrap:
                            to[axis] %= self.sizes[axis]
                        elif not 0 <= to[axis] < self.sizes[axis]:
                            continue
                        hops.append((self.number(x, c, z, y), self.number(**to)))
        return hops

    def number(self, x, c, z, y):
        return ((x * CORES + c) * self.zs + z) * self.ys + y

    def swap(self, values, axis):
        return lax.ppermute(values, AXES, self.shifted(axis, 1, True))

    def along(self, values, axis, step):
        return lax.ppermute(values, AXES, self.shifted(axis, step, False))


def line_gather(grid, at, shard):
    up, down = [shard], [shard]
    for _ in range(grid.zs - 1):
        up.append(grid.along(up[-1], "z", 1))
        down.append(grid.along(down[-1], "z", -1))
    line = jnp.stack(up[:0:-1] + [shard] + down[1:])
    return lax.dynamic_slice_in_dim(line, grid.zs - 1 - at["z"], grid.zs, 0)


def own_swaps(grid, block, first, second):
    return grid.swap(block, first), grid.swap(block, second)


def pair_gather(grid, block, swapped, first, second):
    near, far = swapped
    pieces = {(0, 0): block, (1, 0): near, (0, 1): far, (1, 1): grid.swap(near, second)}
    found = {}
    for (one, two), piece in pieces.items():
        flips = {first: one, second: two}
        found[(flips["x"], 0, flips["y"])] = piece
        found[(flips["x"], 1, flips["y"])] = grid.swap(piece, "c")
    return found


def assemble_kernel(plan, grid, count, outs, spot, *refs):
    pieces, whole, sem = refs[:count], refs[count : count + outs], refs[-1]
    copies = []
    for source, (flip, out, rows, columns, start) in enumerate_plan(plan):
        x, c, y = ((spot[i] + flip[i]) % 2 for i in range(3))
        copies.append(
            pltpu.make_async_copy(
                pieces[source].at[:, pl.ds(start, rows), :],
                whole[out].at[x, c, :, y, :, pl.ds(columns[0], columns[1])],
                sem.at[len(copies)],
            )
        )
    for copy in copies:
        copy.start()
    for copy in copies:
        copy.wait()


def enumerate_plan(plan):
    for source, (flip, targets) in enumerate(plan):
        for out, rows, columns, start in targets:
            yield source, (flip, out, rows, columns, start)


def assemble(grid, at, parts, shapes):
    plan, arrays = [], []
    for pieces, targets in parts:
        for flip, piece in pieces.items():
            plan.append((flip, targets))
            arrays.append(piece)
    copies = sum(len(targets) for _, targets in plan)
    spot = jnp.stack([at["x"], at["c"], at["y"]]).astype(jnp.int32)
    outs = [
        jax.ShapeDtypeStruct((grid.xs, CORES, grid.zs, grid.ys) + shape, jnp.bfloat16)
        for shape in shapes
    ]
    size = sum(2 * piece.size for piece in arrays)
    whole = pl.pallas_call(
        functools.partial(assemble_kernel, plan, grid, len(arrays), len(outs)),
        out_shape=outs,
        in_specs=[pl.BlockSpec(memory_space=pltpu.SMEM)]
        + [pl.BlockSpec(memory_space=pl.ANY)] * len(arrays),
        out_specs=[pl.BlockSpec(memory_space=pl.ANY)] * len(outs),
        scratch_shapes=[pltpu.SemaphoreType.DMA((copies,))],
        cost_estimate=pl.CostEstimate(flops=0, bytes_accessed=2 * size, transcendentals=0),
        compiler_params=pltpu.CompilerParams(vmem_limit_bytes=1 << 20),
    )(spot, *arrays)
    return [w.reshape(grid.count * s[0], s[1]) for w, s in zip(whole, shapes)]


def take(values, index, axis):
    return lax.dynamic_index_in_dim(values, index, axis, keepdims=False)


def total(terms):
    result = terms[0].astype(jnp.float32)
    for term in terms[1:]:
        result = result + term.astype(jnp.float32)
    return result


class Chain:
    def __init__(self, grid, at, sent, kept):
        self.grid, self.at = grid, at
        got = grid.swap(sent, "c")
        shape = (grid.xs, grid.zs, grid.ys, -1, sent.shape[1])
        self.terms = [kept.reshape(shape), got.reshape(shape)]
        self.cut = sent.shape[1] // 256 * 128

    def first(self):
        self.left = [term[..., : self.cut] for term in self.terms]
        self.right = [term[..., self.cut :] for term in self.terms]
        return self.give("x", 0, "y", 2)

    def give(self, left_name, left_axis, right_name, right_axis):
        self.names = (left_name, left_axis, right_name, right_axis)
        sent = []
        for terms, name, axis in (
            (self.left, left_name, left_axis),
            (self.right, right_name, right_axis),
        ):
            values = total([take(term, 1 - self.at[name], axis) for term in terms])
            sent.append(values.astype(jnp.bfloat16))
        return tuple(sent)

    def get(self, sent):
        left_name, left_axis, right_name, right_axis = self.names
        self.left = [take(term, self.at[left_name], left_axis) for term in self.left]
        self.left.append(self.grid.swap(sent[0], left_name))
        self.right = [take(term, self.at[right_name], right_axis) for term in self.right]
        self.right.append(self.grid.swap(sent[1], right_name))

    def second(self, sent):
        self.get(sent)
        return self.give("y", 1, "x", 0)

    def line(self, sent):
        self.get(sent)
        joined = jnp.concatenate([total(self.left), total(self.right)], axis=-1)
        return joined.astype(jnp.bfloat16)


def line_reduce(grid, at, block):
    size = grid.zs

    def own(index):
        return take(block, jnp.clip(index, 0, size - 1), 0).astype(jnp.float32)

    up = low = None
    for step in range(1, size):
        up_sum, low_sum = own(at["z"] + size - step), own(at["z"] - size + step)
        if step > 1:
            up_sum, low_sum = up_sum + up.astype(jnp.float32), low_sum + low.astype(jnp.float32)
        up = grid.along(up_sum.astype(jnp.bfloat16), "z", 1)
        low = grid.along(low_sum.astype(jnp.bfloat16), "z", -1)
    return own(at["z"]) + up.astype(jnp.float32) + low.astype(jnp.float32)


def by_halves(parts):
    return jnp.concatenate([p[:, i : i + HALF] for i in (0, HALF) for p in parts], axis=1)


def pack_small(smalls, rows):
    flat = jnp.concatenate(smalls)
    return jnp.pad(flat, (0, rows * 128 - flat.size)).reshape(rows, 128)


def gather_first(grid, at, attn, smalls):
    rows = attn[0].shape[0]
    line = line_gather(
        grid, at, jnp.concatenate([by_halves(attn), pack_small(smalls, rows)], axis=1)
    )
    return line


def gather_attention(grid, at, line, rows):
    columns = line.shape[2]
    cut = (columns // 256) * 128
    left, right = line[:, :, :cut], line[:, :, cut:]
    left = pair_gather(grid, left, own_swaps(grid, left, "y", "x"), "y", "x")
    right = pair_gather(grid, right, own_swaps(grid, right, "x", "y"), "x", "y")
    (full,) = assemble(
        grid,
        at,
        [(left, [(0, rows, (0, cut), 0)]), (right, [(0, rows, (cut, columns - cut), 0)])],
        [(rows, columns)],
    )
    return full[:, : 3 * D], full[:, 3 * D :].reshape(grid.count, -1)


def gather_rest(grid, at, line, swaps, rows, lower, wide):
    split = rows + lower
    down_part = pair_gather(grid, line[:, :split], swaps[0], "y", "x")
    up_part = pair_gather(grid, line[:, split:], swaps[1], "x", "y")
    up_targets = [(1, rows, (i * D, D), i * rows) for i in range(wide // D)]
    return assemble(
        grid,
        at,
        [
            (down_part, [(0, rows, (0, D), 0), (2, lower, (0, D), rows)]),
            (up_part, up_targets),
        ],
        [(rows, D), (rows, wide), (lower, D)],
    )


def split_small(small, widths):
    results, start = [], 0
    for width in widths:
        results.append(small[:, start : start + width].reshape(-1).astype(jnp.float32))
        start += width
    return results


def hold(later, *ready):
    return lax.optimization_barrier((later, *ready))


def halves(parts, right):
    return tuple(outer_sum(parts[i], right).astype(jnp.bfloat16) for i in range(2))


def plain_reduce(grid, parts, right):
    both = [outer_sum(parts[i], right).reshape(grid.xs, -1, right.shape[1]) for i in (1, 0)]
    whole = jnp.stack(both, axis=1).reshape(-1, right.shape[1])
    return lax.psum_scatter(whole, AXES, scatter_dimension=0, tiled=True)


def per_device(
    grid,
    tokens,
    segment_ids,
    w_query,
    b_query,
    w_key,
    w_value,
    b_value,
    w_out,
    b_out,
    ln1_gain,
    ln1_bias,
    w_up,
    b_up,
    w_down,
    b_down,
    ln2_gain,
    ln2_bias,
    out_cotangent,
):
    at = grid.at()
    rows, wide = w_up.shape
    lower = w_down.shape[0]
    smalls = (b_query, b_value, b_out, ln1_gain, ln1_bias, b_down, ln2_gain, ln2_bias, b_up)
    widths = [small.shape[0] for small in smalls]
    attn = (w_query, w_key, w_value)
    low_tokens = tokens
    if grid.pairs:
        first = gather_first(grid, at, attn, smalls)
        rest = [w_out, w_down] + [w_up[:, i : i + D] for i in range(0, wide, D)]
        rest, first = hold(jnp.concatenate(rest, axis=0), first)
        line = line_gather(grid, at, rest)
        full_qkv, small = gather_attention(grid, at, first, rows)
        low_tokens, line = hold(tokens, line)
        split = rows + lower
        swaps = [
            own_swaps(grid, line[:, :split], "y", "x"),
            own_swaps(grid, line[:, split:], "x", "y"),
        ]
    else:
        full_qkv, full_out, full_up, full_down = (
            lax.all_gather(w, AXES, axis=0, tiled=True)
            for w in (by_halves(attn), w_out, w_up, w_down)
        )
        small = lax.all_gather(jnp.concatenate(smalls), AXES, axis=0, tiled=True)
        small = small.reshape(grid.count, -1)
    bias_query, bias_value, *others, bias_up = split_small(small, widths)
    vectors = jnp.stack(others + [jnp.zeros_like(bias_query)] * 2)
    doc_row, doc_column = segment_ids[:, None, :], segment_ids[:, :, None]
    biases = (bias_query, jnp.zeros_like(bias_query), bias_value)
    bias_qkv = by_halves([bias[None] for bias in biases])
    qkv = (matmul(low_tokens, full_qkv) + bias_qkv).astype(jnp.bfloat16)
    mixed = attend_forward(qkv, doc_column, doc_row)
    if grid.pairs:
        swaps, mixed = hold(swaps, mixed)
        full_out, full_up, full_down = gather_rest(grid, at, line, swaps, rows, lower, wide)
    core = at["c"] if grid.pairs else at["c"] * 0
    blocks = grid.xs * CORES
    (
        output,
        grad_sum,
        grad_low,
        normed,
        scale,
        active_parts,
        slope,
        first_parts,
        mixed_parts,
        token_parts,
        sums_two,
    ) = middle_forward(
        core.reshape(1).astype(jnp.int32),
        blocks,
        mixed,
        tokens,
        out_cotangent,
        full_out,
        full_up,
        full_down,
        vectors,
        bias_up.reshape(1, -1),
    )
    kept = (slope, normed, scale, full_out, full_up, full_down, vectors)
    if grid.pairs:
        down_chain = Chain(grid, at, *halves(active_parts, grad_low))
        down_sent = down_chain.first()
        grad_low, down_sent = hold(grad_low, down_sent)
    grad_up, grad_hidden, branch, grad_mixed, sums_one, sums_up = middle_backward(
        grad_low, grad_sum, *kept
    )
    if grid.pairs:
        up_chain = Chain(grid, at, *halves(first_parts, grad_up))
        down_sent = down_chain.second(down_sent)
        up_sent = up_chain.first()
        grad_mixed, up_sent, down_sent = hold(grad_mixed, up_sent, down_sent)
    one, sums_first = attend_backward(qkv, grad_mixed, doc_column, doc_row, 0)
    if grid.pairs:
        up_sent = up_chain.second(up_sent)
        of_qkv, of_out = halves(token_parts, one), halves(mixed_parts, branch)
        early = [jnp.concatenate([of_qkv[i], of_out[i]], axis=1) for i in range(2)]
        early_chain = Chain(grid, at, *early)
        early_sent = early_chain.first()
        grad_mixed, up_sent, early_sent = hold(grad_mixed, up_sent, early_sent)
    two, sums_second = attend_backward(qkv, grad_mixed, doc_column, doc_row, 1)
    sums_first, sums_second = sums_first[0], sums_second[0]
    totals = [
        jnp.concatenate([sums_first[:HALF], sums_second[:HALF]]),
        jnp.concatenate([sums_first[2 * HALF :], sums_second[2 * HALF :]]),
        sums_one[2],
        sums_one[0],
        sums_one[1],
        sums_up[0],
        sums_two[2],
        sums_two[0],
        sums_two[1],
    ]
    if grid.pairs:
        packed = jnp.concatenate([v.reshape(grid.count, -1) for v in totals], axis=1)
        widths = [v.size // grid.count for v in totals]
        packed = jnp.pad(packed, ((0, 0), (0, rows * 128 - sum(widths)))).astype(jnp.bfloat16)
        packed = packed.reshape(grid.xs, CORES, -1, 128)
        ends = [take(packed, core_at, 1).reshape(-1, 128) for core_at in (1 - at["c"], at["c"])]
        of_qkv = halves(token_parts, two)
        late = [jnp.concatenate([of_qkv[i], ends[i]], axis=1) for i in range(2)]
        late_chain = Chain(grid, at, *late)
        late_sent = late_chain.first()
        two, late_sent = hold(two, late_sent)
        down_block, up_block = down_chain.line(down_sent), up_chain.line(up_sent)
        up_rows = [up_block[:, :, i : i + D] for i in range(0, wide, D)]
        block = line_reduce(grid, at, jnp.concatenate([down_block] + up_rows, axis=1))
        share_down = block[:lower]
        up_rows = [block[i : i + rows] for i in range(lower, lower + rows * wide // D, rows)]
        share_up = jnp.concatenate(up_rows, axis=1)
        early_block = early_chain.line(early_chain.second(early_sent))
        late_block = late_chain.line(late_chain.second(late_sent))
        block = line_reduce(grid, at, jnp.concatenate([early_block, late_block], axis=2))
        early, share_out = block[:, : 3 * HALF], block[:, 3 * HALF : 5 * HALF]
        late = block[:, 5 * HALF :]
        flat = late[:, 3 * HALF :].reshape(-1)
        shares, start = [], 0
        for width in widths:
            shares.append(flat[start : start + width])
            start += width
    else:
        share_down = plain_reduce(grid, active_parts, grad_low)
        share_up = plain_reduce(grid, first_parts, grad_up)
        share_out = plain_reduce(grid, mixed_parts, branch)
        early, late = plain_reduce(grid, token_parts, one), plain_reduce(grid, token_parts, two)
        shares = [lax.psum_scatter(v, AXES, scatter_dimension=0, tiled=True) for v in totals]
    share_query, share_key, share_value = (
        jnp.concatenate([part[:, i : i + HALF] for part in (early, late)], axis=1)
        for i in range(0, 3 * HALF, HALF)
    )
    tokens_grad = (
        grad_hidden
        + back_matmul(one, full_qkv[:, : 3 * HALF])
        + back_matmul(two, full_qkv[:, 3 * HALF :])
    ).astype(jnp.bfloat16)
    return (
        output,
        tokens_grad,
        share_query,
        shares[0],
        share_key,
        share_value,
        shares[1],
        share_out,
        *shares[2:5],
        share_up,
        shares[5],
        share_down,
        *shares[6:],
    )


def solution(mesh):
    rows, flat = P(AXES, None), P(AXES)
    in_specs = (rows,) * 3 + (flat, rows, rows, flat, rows, flat, flat, flat, rows, flat, rows)
    in_specs += (flat,) * 3 + (rows,)
    out_specs = (rows,) * 3 + (flat, rows, rows, flat, rows, flat, flat, flat, rows, flat, rows)
    out_specs += (flat,) * 3
    return jax.shard_map(
        functools.partial(per_device, Grid(mesh)),
        mesh=mesh,
        in_specs=in_specs,
        out_specs=out_specs,
        check_vma=False,
    )
```

```python
import functools

import jax
import jax.numpy as jnp
from jax import lax
from jax.experimental import pallas as pl
from jax.experimental.pallas import tpu as pltpu
from jax.sharding import PartitionSpec as P

D = 1024
H = 16
DH = 64
SEQ_LEN = 512
AXES = ("dp", "fsdp")
CORES = 2


def matmul(operand, other):
    return jnp.dot(operand, other, preferred_element_type=jnp.float32)


def back_matmul(operand, other):
    return lax.dot_general(
        operand, other, (((1,), (1,)), ((), ())), preferred_element_type=jnp.float32
    )


def outer_sum(operand, other):
    return lax.dot_general(
        operand, other, (((0,), (0,)), ((), ())), preferred_element_type=jnp.float32
    )


def column_sum(values):
    return jnp.sum(values.astype(jnp.float32), axis=0)


def norm_forward(hidden):
    centred = hidden - jnp.mean(hidden, axis=-1, keepdims=True)
    scale_row = lax.rsqrt(jnp.mean(centred * centred, axis=-1, keepdims=True) + 1e-12)
    return (centred * scale_row, scale_row)


def norm_backward(grad_out, normed, scale_row, scaling):
    scaled = grad_out * scaling
    return scale_row * (
        scaled
        - jnp.mean(scaled, axis=-1, keepdims=True)
        - normed * jnp.mean(scaled * normed, axis=-1, keepdims=True)
    )


def across(operand, other):
    return lax.dot_general(
        operand, other, (((1,), (1,)), ((), ())), preferred_element_type=jnp.float32
    )


def down(operand, other):
    return lax.dot_general(
        operand, other, (((0,), (0,)), ((), ())), preferred_element_type=jnp.float32
    )


def attend_forward_kernel(query, key, value, doc_column, doc_row, mixed):
    same = doc_column[0] == doc_row[0]
    heads = []
    for head in range(2):
        lanes = slice(head * DH, (head + 1) * DH)
        scores = across(key[:, lanes], query[:, lanes] * jnp.bfloat16(0.125))
        scores = jnp.where(same, scores, -1000000000.0)
        powers = jnp.exp(scores - jnp.max(scores, axis=0, keepdims=True))
        row_total = jnp.sum(powers, axis=0, keepdims=True)
        heads.append(down(value[:, lanes], powers.astype(jnp.bfloat16)) * (1.0 / row_total))
    mixed[...] = jnp.concatenate(heads, axis=0).T.astype(jnp.bfloat16)


def attend_backward_kernel(query, key, value, grad, doc_column, doc_row, out, sums):
    same = doc_column[0] == doc_row[0]
    step = pl.program_id(1)
    found = ([], [], [])
    for head in range(2):
        lanes = slice(head * DH, (head + 1) * DH)
        scaled = query[:, lanes] * jnp.bfloat16(0.125)
        scores = jnp.where(same, across(key[:, lanes], scaled), -1000000000.0)
        powers = jnp.exp(scores - jnp.max(scores, axis=0, keepdims=True))
        probability = powers * (1.0 / jnp.sum(powers, axis=0, keepdims=True))
        grad_prob = across(value[:, lanes], grad[:, lanes])
        delta = jnp.sum(probability * grad_prob, axis=0, keepdims=True)
        grad_scores = (probability * (grad_prob - delta)).astype(jnp.bfloat16)
        found[0].append(down(key[:, lanes], grad_scores) * 0.125)
        found[1].append(matmul(grad_scores, scaled))
        found[2].append(matmul(probability.astype(jnp.bfloat16), grad[:, lanes]))
    grads = (
        jnp.concatenate(found[0], axis=0).T,
        jnp.concatenate(found[1], axis=1),
        jnp.concatenate(found[2], axis=1),
    )
    first = pl.program_id(0) == 0
    for index, value_of in enumerate(grads):
        rounded = value_of.astype(jnp.bfloat16)
        place = pl.ds(pl.multiple_of(index * HALF + step * 128, 128), 128)
        out[:, place] = rounded
        if index != 1:
            more = jnp.sum(rounded.astype(jnp.float32), axis=0, keepdims=True)
            sums[:, place] = jnp.where(first, 0.0, sums[:, place]) + more


HALF = D // 2
PAIRS = HALF // 128


def head_specs(start):
    def block(part):
        def index(seq, pair):
            pair = pair + start
            return seq, pair // PAIRS * (3 * PAIRS) + part * PAIRS + pair % PAIRS

        return pl.BlockSpec((SEQ_LEN, 128), index)

    docs = [
        pl.BlockSpec((1, SEQ_LEN, 1), lambda seq, pair: (seq, 0, 0)),
        pl.BlockSpec((1, 1, SEQ_LEN), lambda seq, pair: (seq, 0, 0)),
    ]
    return [block(i) for i in range(3)], docs


def attend_forward(qkv, doc_column, doc_row):
    seqs = doc_row.shape[0]
    heads, docs = head_specs(0)
    work = seqs * H * SEQ_LEN * SEQ_LEN
    return pl.pallas_call(
        attend_forward_kernel,
        grid=(seqs, 2 * PAIRS),
        out_shape=jax.ShapeDtypeStruct((seqs * SEQ_LEN, D), jnp.bfloat16),
        in_specs=heads + docs,
        out_specs=pl.BlockSpec((SEQ_LEN, 128), lambda seq, pair: (seq, pair)),
        cost_estimate=pl.CostEstimate(
            flops=16 * DH * work, bytes_accessed=8 * qkv.size, transcendentals=work
        ),
        compiler_params=pltpu.CompilerParams(vmem_limit_bytes=40 << 20),
    )(qkv, qkv, qkv, doc_column, doc_row)


def attend_backward(qkv, grad_mixed, doc_column, doc_row, half):
    seqs = doc_row.shape[0]
    heads, docs = head_specs(half * PAIRS)
    work = seqs * H * SEQ_LEN * SEQ_LEN // 2
    return pl.pallas_call(
        attend_backward_kernel,
        grid=(seqs, PAIRS),
        out_shape=[
            jax.ShapeDtypeStruct((seqs * SEQ_LEN, 3 * HALF), jnp.bfloat16),
            jax.ShapeDtypeStruct((1, 3 * HALF), jnp.float32),
        ],
        in_specs=heads
        + [pl.BlockSpec((SEQ_LEN, 128), lambda seq, pair: (seq, half * PAIRS + pair))]
        + docs,
        out_specs=[
            pl.BlockSpec((SEQ_LEN, 3 * HALF), lambda seq, pair: (seq, 0)),
            pl.BlockSpec((1, 3 * HALF), lambda seq, pair: (0, 0)),
        ],
        cost_estimate=pl.CostEstimate(
            flops=40 * DH * work, bytes_accessed=8 * qkv.size, transcendentals=work
        ),
        compiler_params=pltpu.CompilerParams(vmem_limit_bytes=50 << 20),
    )(qkv, qkv, qkv, grad_mixed, doc_column, doc_row)


CHUNK = 512
TILE = 256


def part_out(core, values, parted, blocks):
    width = values.shape[1] // blocks
    for block in range(blocks):
        half = (block % 2 + core + 1) % 2
        start = block // 2 * width
        parted[half, :, start : start + width] = values[:, block * width : (block + 1) * width]


def load(plan, spot, pieces, whole, sem):
    copies = []
    for source, flip, out, rows, columns, start in plan:
        if flip is None:
            target = whole[out]
        else:
            x, c, y = ((spot[i] + flip[i]) % 2 for i in range(3))
            target = whole[out].at[x, c, :, y, :, pl.ds(columns[0], columns[1])]
        part = pieces[source] if flip is None else pieces[source].at[:, pl.ds(start, rows), :]
        copies.append(pltpu.make_async_copy(part, target, sem.at[len(copies)]))
    return copies


def fetch(plan, spot, pieces, whole, sem):
    @pl.when(pl.program_id(0) == 0)
    def _():
        copies = load(plan, spot, pieces, whole, sem)
        for copy in copies:
            copy.start()
        for copy in copies:
            copy.wait()


def columns_of(weight, start, size):
    return weight[..., start : start + size].reshape(-1, size)


def block_of(weight, block):
    return weight[block // CORES, block % CORES].reshape(-1, weight.shape[-1])


def middle_up_kernel(plan, blocks, count, spot, *refs):
    pieces, refs = refs[:count], refs[count:]
    mixed, tokens, vectors, bias_up = refs[:4]
    first_full, normed, scale, active_parts, slope, first_parts, mixed_parts, token_parts = refs[4:12]
    w_out, w_up, sem = refs[12:]
    fetch(plan, spot, pieces, (w_out, w_up), sem)
    core = spot[1]
    bias_out, gain_one, shift_one = (vectors[i : i + 1, :] for i in range(3))
    part_out(core, mixed[...], mixed_parts, blocks)
    part_out(core, tokens[...], token_parts, blocks)
    hidden = tokens[...].astype(jnp.float32) + matmul(mixed[...], columns_of(w_out, 0, D)) + bias_out
    normed_one, scale_one = norm_forward(hidden)
    normed[...] = normed_one
    scale[...] = jnp.broadcast_to(scale_one, scale.shape)
    first_out = normed_one * gain_one + shift_one
    first_full[...] = first_out
    first_low = first_out.astype(jnp.bfloat16)
    part_out(core, first_low, first_parts, blocks)
    wide = w_up.shape[-1]
    width = wide // blocks
    for start in range(0, wide, CHUNK):
        at = slice(start, start + CHUNK)
        upward = matmul(first_low, columns_of(w_up, start, CHUNK)) + bias_up[:, at]
        phi = 0.5 * (1.0 + lax.erf(upward * 0.7071067811865476))
        active = (upward * phi).astype(jnp.bfloat16)
        slope[:, at] = (
            phi + upward * jnp.exp(-0.5 * upward * upward) * 0.3989422804014327
        ).astype(jnp.bfloat16)
        block, inside = start // width, start % width
        half = (block % 2 + core + 1) % 2
        place = block // 2 * width + inside
        active_parts[half, :, place : place + CHUNK] = active


def middle_down_kernel(plan, blocks, count, spot, *refs):
    pieces, refs = refs[:count], refs[count:]
    first_full, active_parts, cotangent, vectors = refs[:4]
    output, grad_sum, grad_low, sums, w_down, sem = refs[4:]
    fetch(plan, spot, pieces, (w_down,), sem)
    bias_down, gain_two, shift_two = (vectors[i : i + 1, :] for i in range(3, 6))
    second = first_full[...] + bias_down
    width = active_parts.shape[2] * 2 // blocks
    for block in range(blocks):
        half = (block % 2 + spot[1] + 1) % 2
        place = block // 2 * width
        part = active_parts[half, :, place : place + width]
        second = second + matmul(part, block_of(w_down, block))
    normed_two, scale_two = norm_forward(second)
    output[...] = (normed_two * gain_two + shift_two).astype(jnp.bfloat16)
    grad = cotangent[...]
    grad_second = norm_backward(grad, normed_two, scale_two, gain_two)
    grad_sum[...] = grad_second
    rounded = grad_second.astype(jnp.bfloat16)
    grad_low[...] = rounded

    @pl.when(pl.program_id(0) == 0)
    def _():
        sums[...] = jnp.zeros_like(sums)

    sums[0:1, :] += jnp.sum(grad * normed_two, axis=0, keepdims=True)
    sums[1:2, :] += jnp.sum(grad, axis=0, keepdims=True)
    sums[2:3, :] += jnp.sum(rounded.astype(jnp.float32), axis=0, keepdims=True)


def middle_backward_kernel(plan, count, spot, *refs):
    pieces, refs = refs[:count], refs[count:]
    grad_low, grad_sum, slope, normed, scale, vectors = refs[:6]
    grad_up, grad_hidden, branch, grad_mixed, sums, sums_up = refs[6:12]
    w_out, w_up, w_down, sem = refs[12:]
    fetch(plan, spot, pieces, (w_out, w_up, w_down), sem)

    @pl.when(pl.program_id(0) == 0)
    def _():
        sums[...] = jnp.zeros_like(sums)
        sums_up[...] = jnp.zeros_like(sums_up)

    grad_first = grad_sum[...]
    low = grad_low[...]
    wide = w_up.shape[-1]
    width = wide // (w_down.shape[0] * w_down.shape[1])
    for start in range(0, wide, CHUNK):
        at = slice(start, start + CHUNK)
        rows = block_of(w_down, start // width)[start % width : start % width + CHUNK]
        part = (across(low, rows) * slope[:, at].astype(jnp.float32)).astype(jnp.bfloat16)
        grad_up[:, at] = part
        sums_up[:, at] += jnp.sum(part.astype(jnp.float32), axis=0, keepdims=True)
        grad_first = grad_first + across(part, columns_of(w_up, start, CHUNK))
    normed_one = normed[...]
    sums[0:1, :] += jnp.sum(grad_first * normed_one, axis=0, keepdims=True)
    sums[1:2, :] += jnp.sum(grad_first, axis=0, keepdims=True)
    hidden = norm_backward(grad_first, normed_one, scale[:, 0:1], vectors[1:2, :])
    grad_hidden[...] = hidden
    rounded = hidden.astype(jnp.bfloat16)
    branch[...] = rounded
    sums[2:3, :] += jnp.sum(rounded.astype(jnp.float32), axis=0, keepdims=True)
    grad_mixed[...] = across(rounded, columns_of(w_out, 0, D)).astype(jnp.bfloat16)


def tiled(columns):
    return pl.BlockSpec((TILE, columns), lambda i: (i, 0))


def parted(columns):
    return pl.BlockSpec((2, TILE, columns), lambda i: (0, i, 0))


def resident(shape):
    return pl.BlockSpec(shape, lambda i: (0,) * len(shape), pipeline_mode=pl.Buffered(1))


def middle_call(kernel, grid, spot, weights, tiles, fixed, outs, sums, flops, exps=0):
    arrays, plan, shapes = weights
    rows = tiles[0].shape[-2]
    lead = (grid.xs, CORES, grid.zs, grid.ys)

    def spec(shape):
        return parted(shape[2]) if len(shape) == 3 else tiled(shape[1])

    return pl.pallas_call(
        functools.partial(kernel, plan),
        grid=(rows // TILE,),
        out_shape=[jax.ShapeDtypeStruct(*o) for o in outs]
        + [jax.ShapeDtypeStruct(o, jnp.float32) for o in sums],
        in_specs=[pl.BlockSpec(memory_space=pltpu.SMEM)]
        + [pl.BlockSpec(memory_space=pl.ANY)] * len(arrays)
        + [spec(t.shape) for t in tiles]
        + [resident(f.shape) for f in fixed],
        out_specs=[spec(o[0]) for o in outs] + [pl.BlockSpec(o, lambda i: (0, 0)) for o in sums],
        scratch_shapes=[pltpu.VMEM(lead + shape, jnp.bfloat16) for shape in shapes]
        + [pltpu.SemaphoreType.DMA((len(plan),))],
        cost_estimate=pl.CostEstimate(flops=flops, bytes_accessed=40 << 20, transcendentals=exps),
        compiler_params=pltpu.CompilerParams(vmem_limit_bytes=60 << 20),
    )(spot, *arrays, *tiles, *fixed)


def joined(*weights):
    arrays, plan, shapes = [], [], []
    for some, steps, sizes in weights:
        for source, flip, out, rows, columns, start in steps:
            place = (source + len(arrays), flip, out + len(shapes), rows, columns, start)
            plan.append(place)
        arrays, shapes = arrays + list(some), shapes + list(sizes)
    return arrays, plan, shapes


def middle_up(grid, spot, weights, mixed, tokens, vectors, bias_up):
    rows, wide = tokens.shape[0], bias_up.shape[1]
    outs = [
        ((rows, D), jnp.float32),
        ((rows, D), jnp.float32),
        ((rows, 128), jnp.float32),
        ((2, rows, wide // 2), jnp.bfloat16),
        ((rows, wide), jnp.bfloat16),
        ((2, rows, D // 2), jnp.bfloat16),
        ((2, rows, D // 2), jnp.bfloat16),
        ((2, rows, D // 2), jnp.bfloat16),
    ]

    def kernel(plan, *refs):
        middle_up_kernel(plan, grid.xs * CORES, len(weights[0]), *refs)

    flops = 2 * rows * D * (D + wide)
    return middle_call(
        kernel, grid, spot, weights, [mixed, tokens], [vectors, bias_up], outs, [], flops, 2 * rows * wide
    )


def middle_down(grid, spot, weights, first_full, active_parts, cotangent, vectors):
    rows, wide = first_full.shape[0], active_parts.shape[2] * 2
    outs = [((rows, D), jnp.bfloat16), ((rows, D), jnp.float32), ((rows, D), jnp.bfloat16)]

    def kernel(plan, *refs):
        middle_down_kernel(plan, grid.xs * CORES, len(weights[0]), *refs)

    tiles = [first_full, active_parts, cotangent]
    flops = 2 * rows * D * wide
    return middle_call(kernel, grid, spot, weights, tiles, [vectors], outs, [(8, D)], flops)


def middle_backward(grid, spot, weights, grad_low, grad_sum, slope, normed, scale, vectors):
    rows, wide = slope.shape
    outs = [
        ((rows, wide), jnp.bfloat16),
        ((rows, D), jnp.float32),
        ((rows, D), jnp.bfloat16),
        ((rows, D), jnp.bfloat16),
    ]

    def kernel(plan, *refs):
        middle_backward_kernel(plan, len(weights[0]), *refs)

    tiles = [grad_low, grad_sum, slope, normed, scale]
    flops = 2 * rows * D * (D + 2 * wide)
    return middle_call(
        kernel, grid, spot, weights, tiles, [vectors], outs, [(8, D), (1, wide)], flops
    )


class Grid:
    def __init__(self, mesh):
        self.shape = dict(mesh.shape)
        self.xs = self.shape["dp"] // CORES
        self.ys = self.xs
        self.zs = self.shape["fsdp"] // self.ys
        self.sizes = {"x": self.xs, "c": CORES, "z": self.zs, "y": self.ys}
        self.count = self.shape["dp"] * self.shape["fsdp"]
        self.pairs = self.xs == 2 and self.ys == 2 and self.zs == 4

    def at(self):
        dp, fsdp = lax.axis_index("dp"), lax.axis_index("fsdp")
        return {"x": dp // CORES, "c": dp % CORES, "z": fsdp // self.ys, "y": fsdp % self.ys}

    def shifted(self, axis, step, wrap):
        hops = []
        for x in range(self.xs):
            for c in range(CORES):
                for z in range(self.zs):
                    for y in range(self.ys):
                        to = {"x": x, "c": c, "z": z, "y": y}
                        to[axis] += step
                        if wrap:
                            to[axis] %= self.sizes[axis]
                        elif not 0 <= to[axis] < self.sizes[axis]:
                            continue
                        hops.append((self.number(x, c, z, y), self.number(**to)))
        return hops

    def number(self, x, c, z, y):
        return ((x * CORES + c) * self.zs + z) * self.ys + y

    def swap(self, values, axis):
        return lax.ppermute(values, AXES, self.shifted(axis, 1, True))

    def along(self, values, axis, step):
        return lax.ppermute(values, AXES, self.shifted(axis, step, False))


def place_kernel(steps, count, spot, *refs):
    arrays, out, sem = refs[:count], refs[count], refs[count + 1]

    def each(act):
        for index, (source, select, target, valid) in enumerate(steps):
            def run(index=index, source=source, select=select, target=target):
                part = arrays[source] if select is None else arrays[source].at[select]
                act(pltpu.make_async_copy(part, out.at[target(spot)], sem.at[index]))

            if valid is None:
                run()
            else:
                pl.when(valid(spot))(run)

    each(lambda copy: copy.start())
    each(lambda copy: copy.wait())


def place(arrays, spot, steps, shape):
    size = 4 * sum(a.size for a in arrays)
    return pl.pallas_call(
        functools.partial(place_kernel, steps, len(arrays)),
        out_shape=jax.ShapeDtypeStruct(shape, jnp.bfloat16),
        in_specs=[pl.BlockSpec(memory_space=pltpu.SMEM)]
        + [pl.BlockSpec(memory_space=pl.ANY)] * len(arrays),
        out_specs=pl.BlockSpec(memory_space=pl.ANY),
        scratch_shapes=[pltpu.SemaphoreType.DMA((len(steps),))],
        cost_estimate=pl.CostEstimate(flops=0, bytes_accessed=size, transcendentals=0),
        compiler_params=pltpu.CompilerParams(vmem_limit_bytes=1 << 20),
    )(spot, *arrays)


def line_gather(grid, spot, shard):
    arrays = [shard]
    steps = [(0, None, lambda spot: spot[3], None)]
    up = low = shard
    for hop in range(1, grid.zs):
        up, low = grid.along(up, "z", 1), grid.along(low, "z", -1)
        arrays += [up, low]
        last = grid.zs - 1
        steps.append(
            (
                2 * hop - 1,
                None,
                lambda spot, hop=hop: jnp.maximum(spot[3] - hop, 0),
                lambda spot, hop=hop: spot[3] >= hop,
            )
        )
        steps.append(
            (
                2 * hop,
                None,
                lambda spot, hop=hop: jnp.minimum(spot[3] + hop, last),
                lambda spot, hop=hop: spot[3] + hop <= last,
            )
        )
    return place(arrays, spot, steps, (grid.zs,) + shard.shape)


def own_swaps(grid, block, first, second):
    return grid.swap(block, first), grid.swap(block, second)


def pair_gather(grid, block, swapped, first, second):
    near, far = swapped
    pieces = {(0, 0): block, (1, 0): near, (0, 1): far, (1, 1): grid.swap(near, second)}
    found = {}
    for (one, two), piece in pieces.items():
        flips = {first: one, second: two}
        found[(flips["x"], 0, flips["y"])] = piece
        found[(flips["x"], 1, flips["y"])] = grid.swap(piece, "c")
    return found


def block_plan(parts):
    plan, arrays = [], []
    for pieces, targets in parts:
        for flip, piece in pieces.items():
            for out, rows, columns, start in targets:
                plan.append((len(arrays), flip, out, rows, columns, start))
            arrays.append(piece)
    return arrays, plan


def assemble_kernel(plan, count, spot, *refs):
    copies = load(plan, spot, refs[:count], refs[count:-1], refs[-1])
    for copy in copies:
        copy.start()
    for copy in copies:
        copy.wait()


def assemble(grid, spot, parts, shape):
    arrays, plan = block_plan(parts)
    size = sum(2 * piece.size for piece in arrays)
    whole = pl.pallas_call(
        functools.partial(assemble_kernel, plan, len(arrays)),
        out_shape=jax.ShapeDtypeStruct((grid.xs, CORES, grid.zs, grid.ys) + shape, jnp.bfloat16),
        in_specs=[pl.BlockSpec(memory_space=pltpu.SMEM)]
        + [pl.BlockSpec(memory_space=pl.ANY)] * len(arrays),
        out_specs=pl.BlockSpec(memory_space=pl.ANY),
        scratch_shapes=[pltpu.SemaphoreType.DMA((len(plan),))],
        cost_estimate=pl.CostEstimate(flops=0, bytes_accessed=2 * size, transcendentals=0),
        compiler_params=pltpu.CompilerParams(vmem_limit_bytes=1 << 20),
    )(spot, *arrays)
    return whole.reshape(grid.count * shape[0], shape[1])


def take(values, index, axis):
    return lax.dynamic_index_in_dim(values, index, axis, keepdims=False)


def total(terms):
    result = terms[0].astype(jnp.float32)
    for term in terms[1:]:
        result = result + term.astype(jnp.float32)
    return result


class Chain:
    def __init__(self, grid, at, sent, kept):
        self.grid, self.at = grid, at
        got = grid.swap(sent, "c")
        shape = (grid.xs, grid.zs, grid.ys, -1, sent.shape[1])
        terms = [kept.reshape(shape), got.reshape(shape)]
        cut = sent.shape[1] // 256 * 128
        self.sides = [[t[..., :cut] for t in terms], [t[..., cut:] for t in terms]]

    def give(self, *ways):
        self.ways = ways
        sent = []
        for terms, (name, axis) in zip(self.sides, ways):
            values = total([take(term, 1 - self.at[name], axis) for term in terms])
            sent.append(values.astype(jnp.bfloat16))
        return tuple(sent)

    def first(self):
        return self.give(("x", 0), ("y", 2))

    def swap(self, sent):
        return tuple(self.grid.swap(values, way[0]) for values, way in zip(sent, self.ways))

    def get(self, received):
        self.sides = [
            [take(term, self.at[name], axis) for term in terms] + [values]
            for terms, (name, axis), values in zip(self.sides, self.ways, received)
        ]

    def second(self, received):
        self.get(received)
        return self.give(("y", 1), ("x", 0))

    def block(self, received):
        self.get(received)
        return jnp.concatenate([total(terms) for terms in self.sides], axis=-1).astype(jnp.bfloat16)


class Line:
    def __init__(self, grid, at, block):
        self.grid, self.at, self.block = grid, at, block

    def own(self, index):
        index = jnp.clip(index, 0, self.grid.zs - 1)
        return take(self.block, index, 0).astype(jnp.float32)

    def give(self, hop, received=None):
        size = self.grid.zs
        sums = [self.own(self.at["z"] + size - hop), self.own(self.at["z"] - size + hop)]
        if received is not None:
            sums = [own + more.astype(jnp.float32) for own, more in zip(sums, received)]
        return tuple(values.astype(jnp.bfloat16) for values in sums)

    def move(self, sent):
        return tuple(self.grid.along(values, "z", step) for values, step in zip(sent, (1, -1)))

    def end(self, received):
        return total([self.own(self.at["z"]), *received])

    def rest(self, received, hop):
        for step in range(hop, self.grid.zs):
            received = self.move(self.give(step, received))
        return self.end(received)


def by_halves(parts):
    return jnp.concatenate([p[:, i : i + HALF] for i in (0, HALF) for p in parts], axis=1)


def pack_small(smalls, rows):
    flat = jnp.concatenate(smalls)
    return jnp.pad(flat, (0, rows * 128 - flat.size)).reshape(rows, 128)


def pack_first(spot, attn, small):
    steps = []
    for half in range(2):
        for part in range(3):
            start = (3 * half + part) * HALF
            steps.append(
                (
                    part,
                    (slice(None), pl.ds(half * HALF, HALF)),
                    lambda spot, start=start: (slice(None), pl.ds(start, HALF)),
                    None,
                )
            )
    steps.append((3, None, lambda spot: (slice(None), pl.ds(3 * D, 128)), None))
    return place([*attn, small], spot, steps, (attn[0].shape[0], 3 * D + 128))


def pack_rest(spot, w_out, w_up, w_down):
    rows, wide = w_up.shape
    steps = [(0, None, lambda spot: (pl.ds(0, rows), slice(None)), None)]
    for i in range(wide // D):
        steps.append(
            (
                1,
                (slice(None), pl.ds(i * D, D)),
                lambda spot, i=i: (pl.ds((i + 1) * rows, rows), slice(None)),
                None,
            )
        )
    start = rows + rows * wide // D
    steps.append((2, None, lambda spot: (pl.ds(start, w_down.shape[0]), slice(None)), None))
    return place([w_out, w_up, w_down], spot, steps, (start + w_down.shape[0], D))


class Gather:
    orders = (("y", "x"), ("x", "y"))

    def __init__(self, grid, line):
        self.grid = grid
        self.cut = line.shape[2] // 256 * 128
        self.columns = line.shape[2]
        self.sides = [line[:, :, : self.cut], line[:, :, self.cut :]]

    def start(self):
        self.swaps = [own_swaps(self.grid, v, *o) for v, o in zip(self.sides, self.orders)]

    def blocks(self):
        return [
            pair_gather(self.grid, v, swapped, *order)
            for v, swapped, order in zip(self.sides, self.swaps, self.orders)
        ]

    def parts(self, targets):
        spans = [(0, self.cut), (self.cut, self.columns - self.cut)]
        return [
            (
                pieces,
                [(out, rows, (first + span[0], span[1]), start) for out, rows, first, start in targets],
            )
            for pieces, span in zip(self.blocks(), spans)
        ]


def split_small(small, widths):
    results, start = [], 0
    for width in widths:
        results.append(small[:, start : start + width].reshape(-1).astype(jnp.float32))
        start += width
    return results


def hold(later, *ready):
    return lax.optimization_barrier((later, *ready))


def halves(parts, right):
    return tuple(outer_sum(parts[i], right).astype(jnp.bfloat16) for i in range(2))


def plain_reduce(grid, parts, right):
    both = [outer_sum(parts[i], right).reshape(grid.xs, -1, right.shape[1]) for i in (1, 0)]
    whole = jnp.stack(both, axis=1).reshape(-1, right.shape[1])
    return lax.psum_scatter(whole, AXES, scatter_dimension=0, tiled=True)


def per_device(
    grid,
    tokens,
    segment_ids,
    w_query,
    b_query,
    w_key,
    w_value,
    b_value,
    w_out,
    b_out,
    ln1_gain,
    ln1_bias,
    w_up,
    b_up,
    w_down,
    b_down,
    ln2_gain,
    ln2_bias,
    out_cotangent,
):
    at = grid.at()
    rows, wide = w_up.shape
    lower = w_down.shape[0]
    smalls = (b_query, b_value, b_out, ln1_gain, ln1_bias, b_down, ln2_gain, ln2_bias, b_up)
    widths = [small.shape[0] for small in smalls]
    attn = (w_query, w_key, w_value)
    low_tokens = tokens
    places = [at[name] for name in "xcyz"]
    spot = jnp.stack(places).astype(jnp.int32)
    if grid.pairs:
        first = line_gather(grid, spot, pack_first(spot, attn, pack_small(smalls, rows)))
        rest = pack_rest(spot, w_out, w_up, w_down)
        rest, first = hold(rest, first)
        gather = Gather(grid, first)
        gather.start()
        whole = assemble(grid, spot, gather.parts([(0, rows, 0, 0)]), (rows, 3 * D + 128))
        full_qkv, small = whole[:, : 3 * D], whole[:, 3 * D :].reshape(grid.count, -1)
        line = line_gather(grid, spot, rest)
        low_tokens, line = hold(tokens, line)
        split = rows + rows * wide // D
        up_gather, down_gather = Gather(grid, line[:, :split]), Gather(grid, line[:, split:])
        up_gather.start()
    else:
        full_qkv, full_out, full_up, full_down = (
            lax.all_gather(w, AXES, axis=0, tiled=True)
            for w in (by_halves(attn), w_out, w_up, w_down)
        )
        small = lax.all_gather(jnp.concatenate(smalls), AXES, axis=0, tiled=True)
        small = small.reshape(grid.count, -1)
    bias_query, bias_value, *others, bias_up = split_small(small, widths)
    vectors = jnp.stack(others + [jnp.zeros_like(bias_query)] * 2)
    doc_row, doc_column = segment_ids[:, None, :], segment_ids[:, :, None]
    biases = (bias_query, jnp.zeros_like(bias_query), bias_value)
    bias_qkv = by_halves([bias[None] for bias in biases])
    qkv = (matmul(low_tokens, full_qkv) + bias_qkv).astype(jnp.bfloat16)
    mixed = attend_forward(qkv, doc_column, doc_row)
    up_shapes, down_shapes = [(rows, D), (rows, wide)], [(lower, D)]
    if grid.pairs:
        up_gather.swaps, mixed = hold(up_gather.swaps, mixed)
        targets = [(0, rows, 0, 0)]
        targets += [(1, rows, i * D, (i + 1) * rows) for i in range(wide // D)]
        up_weights = (*block_plan(up_gather.parts(targets)), up_shapes)
        down_gather.sides, up_weights[0][:] = hold(down_gather.sides, up_weights[0])
        down_gather.start()
    else:
        spot = spot * 0
        lead = (grid.xs, CORES, grid.zs, grid.ys)
        up_weights = (
            [full_out.reshape(lead + (rows, D)), full_up.reshape(lead + (rows, wide))],
            [(0, None, 0, rows, None, 0), (1, None, 1, rows, None, 0)],
            up_shapes,
        )
    bias_wide = bias_up.reshape(1, -1)
    (
        first_full,
        normed,
        scale,
        active_parts,
        slope,
        first_parts,
        mixed_parts,
        token_parts,
    ) = middle_up(grid, spot, up_weights, mixed, tokens, vectors, bias_wide)
    if grid.pairs:
        down_gather.swaps, first_full = hold(down_gather.swaps, first_full)
        down_parts = down_gather.parts([(0, lower, 0, 0)])
        down_weights = (*block_plan(down_parts), down_shapes)
    else:
        down_weights = ([full_down.reshape(lead + (lower, D))], [(0, None, 0, lower, None, 0)], down_shapes)
    output, grad_sum, grad_low, sums_two = middle_down(
        grid, spot, down_weights, first_full, active_parts, out_cotangent, vectors
    )
    if grid.pairs:
        down_chain = Chain(grid, at, *halves(active_parts, grad_low))
        grad_low, down_sent = hold(grad_low, down_chain.first())
    made = middle_backward(
        grid, spot, joined(up_weights, down_weights), grad_low, grad_sum, slope, normed, scale, vectors
    )
    grad_up, grad_hidden, branch, grad_mixed, sums_one, sums_up = made
    if grid.pairs:
        received, grad_up, branch, grad_mixed = hold(
            down_chain.swap(down_sent), grad_up, branch, grad_mixed
        )
        down_sent, grad_up = hold(down_chain.second(received), grad_up)
        up_chain = Chain(grid, at, *halves(first_parts, grad_up))
        up_sent, received = hold(up_chain.first(), down_chain.swap(down_sent))
        down_line = Line(grid, at, down_chain.block(received))
        down_sent, up_sent, grad_mixed = hold(down_line.give(1), up_sent, grad_mixed)
    one, sums_first = attend_backward(qkv, grad_mixed, doc_column, doc_row, 0)
    if grid.pairs:
        received, down_got, one, branch, grad_mixed = hold(
            up_chain.swap(up_sent), down_line.move(down_sent), one, branch, grad_mixed
        )
        up_sent, down_sent, one, branch = hold(
            up_chain.second(received), down_line.give(2, down_got), one, branch
        )
        of_qkv, of_out = halves(token_parts, one), halves(mixed_parts, branch)
        early = [jnp.concatenate([of_qkv[i], of_out[i]], axis=1) for i in range(2)]
        early_chain = Chain(grid, at, *early)
        early_sent, received, down_got = hold(
            early_chain.first(), up_chain.swap(up_sent), down_line.move(down_sent)
        )
        up_line = Line(grid, at, up_chain.block(received))
        up_sent, down_sent, early_sent, grad_mixed = hold(
            up_line.give(1), down_line.give(3, down_got), early_sent, grad_mixed
        )
    two, sums_second = attend_backward(qkv, grad_mixed, doc_column, doc_row, 1)
    if grid.pairs:
        received, up_got, down_got, two = hold(
            early_chain.swap(early_sent), up_line.move(up_sent), down_line.move(down_sent), two
        )
        early_sent, up_sent, two = hold(early_chain.second(received), up_line.give(2, up_got), two)
    sums_first, sums_second = sums_first[0], sums_second[0]
    totals = [
        jnp.concatenate([sums_first[:HALF], sums_second[:HALF]]),
        jnp.concatenate([sums_first[2 * HALF :], sums_second[2 * HALF :]]),
        sums_one[2],
        sums_one[0],
        sums_one[1],
        sums_up[0],
        sums_two[2],
        sums_two[0],
        sums_two[1],
    ]
    if grid.pairs:
        share_down = down_line.rest(down_got, grid.zs)
        packed = jnp.concatenate([v.reshape(grid.count, -1) for v in totals], axis=1)
        widths = [v.size // grid.count for v in totals]
        packed = jnp.pad(packed, ((0, 0), (0, rows * 128 - sum(widths)))).astype(jnp.bfloat16)
        packed = packed.reshape(grid.xs, CORES, -1, 128)
        ends = [take(packed, core_at, 1).reshape(-1, 128) for core_at in (1 - at["c"], at["c"])]
        of_qkv = halves(token_parts, two)
        late = [jnp.concatenate([of_qkv[i], ends[i]], axis=1) for i in range(2)]
        late_chain = Chain(grid, at, *late)
        late_sent, received, up_got = hold(
            late_chain.first(), early_chain.swap(early_sent), up_line.move(up_sent)
        )
        two, late_sent = hold(two, late_sent)
        share_up = up_line.rest(up_got, 3)
        early_block = early_chain.block(received)
        late_sent = late_chain.second(late_chain.swap(late_sent))
        late_block = late_chain.block(late_chain.swap(late_sent))
        line = Line(grid, at, jnp.concatenate([early_block, late_block], axis=2))
        block = line.rest(line.move(line.give(1)), 2)
        early, share_out = block[:, : 3 * HALF], block[:, 3 * HALF : 5 * HALF]
        late = block[:, 5 * HALF :]
        flat = late[:, 3 * HALF :].reshape(-1)
        shares, start = [], 0
        for width in widths:
            shares.append(flat[start : start + width])
            start += width
    else:
        share_down = plain_reduce(grid, active_parts, grad_low)
        share_up = plain_reduce(grid, first_parts, grad_up)
        share_out = plain_reduce(grid, mixed_parts, branch)
        early, late = plain_reduce(grid, token_parts, one), plain_reduce(grid, token_parts, two)
        shares = [lax.psum_scatter(v, AXES, scatter_dimension=0, tiled=True) for v in totals]
    share_query, share_key, share_value = (
        jnp.concatenate([part[:, i : i + HALF] for part in (early, late)], axis=1)
        for i in range(0, 3 * HALF, HALF)
    )
    tokens_grad = (
        grad_hidden
        + back_matmul(one, full_qkv[:, : 3 * HALF])
        + back_matmul(two, full_qkv[:, 3 * HALF :])
    ).astype(jnp.bfloat16)
    return (
        output,
        tokens_grad,
        share_query,
        shares[0],
        share_key,
        share_value,
        shares[1],
        share_out,
        *shares[2:5],
        share_up,
        shares[5],
        share_down,
        *shares[6:],
    )


def solution(mesh):
    rows, flat = P(AXES, None), P(AXES)
    in_specs = (rows,) * 3 + (flat, rows, rows, flat, rows, flat, flat, flat, rows, flat, rows)
    in_specs += (flat,) * 3 + (rows,)
    out_specs = (rows,) * 3 + (flat, rows, rows, flat, rows, flat, flat, flat, rows, flat, rows)
    out_specs += (flat,) * 3
    return jax.shard_map(
        functools.partial(per_device, Grid(mesh)),
        mesh=mesh,
        in_specs=in_specs,
        out_specs=out_specs,
        check_vma=False,
    )
```

```python
import functools

import jax
import jax.numpy as jnp
from jax import lax
from jax.experimental import pallas as pl
from jax.experimental.pallas import tpu as pltpu
from jax.sharding import PartitionSpec as P

D = 1024
H = 16
DH = 64
SEQ_LEN = 512
AXES = ("dp", "fsdp")
CORES = 2


def matmul(operand, other):
    return jnp.dot(operand, other, preferred_element_type=jnp.float32)


def back_matmul(operand, other):
    return lax.dot_general(
        operand, other, (((1,), (1,)), ((), ())), preferred_element_type=jnp.float32
    )


def outer_sum(operand, other):
    return lax.dot_general(
        operand, other, (((0,), (0,)), ((), ())), preferred_element_type=jnp.float32
    )


def column_sum(values):
    return jnp.sum(values.astype(jnp.float32), axis=0)


def norm_forward(hidden):
    centred = hidden - jnp.mean(hidden, axis=-1, keepdims=True)
    scale_row = lax.rsqrt(jnp.mean(centred * centred, axis=-1, keepdims=True) + 1e-12)
    return (centred * scale_row, scale_row)


def norm_backward(grad_out, normed, scale_row, scaling):
    scaled = grad_out * scaling
    return scale_row * (
        scaled
        - jnp.mean(scaled, axis=-1, keepdims=True)
        - normed * jnp.mean(scaled * normed, axis=-1, keepdims=True)
    )


def across(operand, other):
    return lax.dot_general(
        operand, other, (((1,), (1,)), ((), ())), preferred_element_type=jnp.float32
    )


def down(operand, other):
    return lax.dot_general(
        operand, other, (((0,), (0,)), ((), ())), preferred_element_type=jnp.float32
    )


def attend_forward_kernel(query, key, value, doc_column, doc_row, mixed):
    same = doc_column[0] == doc_row[0]
    heads = []
    for head in range(2):
        lanes = slice(head * DH, (head + 1) * DH)
        scores = across(key[:, lanes], query[:, lanes] * jnp.bfloat16(0.125))
        scores = jnp.where(same, scores, -1000000000.0)
        powers = jnp.exp(scores - jnp.max(scores, axis=0, keepdims=True))
        row_total = jnp.sum(powers, axis=0, keepdims=True)
        heads.append(down(value[:, lanes], powers.astype(jnp.bfloat16)) * (1.0 / row_total))
    mixed[...] = jnp.concatenate(heads, axis=0).T.astype(jnp.bfloat16)


def attend_backward_kernel(query, key, value, grad, doc_column, doc_row, out, sums):
    same = doc_column[0] == doc_row[0]
    step = pl.program_id(1)
    found = ([], [], [])
    for head in range(2):
        lanes = slice(head * DH, (head + 1) * DH)
        scaled = query[:, lanes] * jnp.bfloat16(0.125)
        scores = jnp.where(same, across(key[:, lanes], scaled), -1000000000.0)
        powers = jnp.exp(scores - jnp.max(scores, axis=0, keepdims=True))
        probability = powers * (1.0 / jnp.sum(powers, axis=0, keepdims=True))
        grad_prob = across(value[:, lanes], grad[:, lanes])
        delta = jnp.sum(probability * grad_prob, axis=0, keepdims=True)
        grad_scores = (probability * (grad_prob - delta)).astype(jnp.bfloat16)
        found[0].append(down(key[:, lanes], grad_scores) * 0.125)
        found[1].append(matmul(grad_scores, scaled))
        found[2].append(matmul(probability.astype(jnp.bfloat16), grad[:, lanes]))
    grads = (
        jnp.concatenate(found[0], axis=0).T,
        jnp.concatenate(found[1], axis=1),
        jnp.concatenate(found[2], axis=1),
    )
    first = pl.program_id(0) == 0
    for index, value_of in enumerate(grads):
        rounded = value_of.astype(jnp.bfloat16)
        place = pl.ds(pl.multiple_of(index * HALF + step * 128, 128), 128)
        out[:, place] = rounded
        if index != 1:
            more = jnp.sum(rounded.astype(jnp.float32), axis=0, keepdims=True)
            sums[:, place] = jnp.where(first, 0.0, sums[:, place]) + more


HALF = D // 2
PAIRS = HALF // 128


def head_specs(start):
    def block(part):
        def index(seq, pair):
            pair = pair + start
            return seq, pair // PAIRS * (3 * PAIRS) + part * PAIRS + pair % PAIRS

        return pl.BlockSpec((SEQ_LEN, 128), index)

    docs = [
        pl.BlockSpec((1, SEQ_LEN, 1), lambda seq, pair: (seq, 0, 0)),
        pl.BlockSpec((1, 1, SEQ_LEN), lambda seq, pair: (seq, 0, 0)),
    ]
    return [block(i) for i in range(3)], docs


def attend_forward(qkv, doc_column, doc_row):
    seqs = doc_row.shape[0]
    heads, docs = head_specs(0)
    work = seqs * H * SEQ_LEN * SEQ_LEN
    return pl.pallas_call(
        attend_forward_kernel,
        grid=(seqs, 2 * PAIRS),
        out_shape=jax.ShapeDtypeStruct((seqs * SEQ_LEN, D), jnp.bfloat16),
        in_specs=heads + docs,
        out_specs=pl.BlockSpec((SEQ_LEN, 128), lambda seq, pair: (seq, pair)),
        cost_estimate=pl.CostEstimate(
            flops=16 * DH * work, bytes_accessed=8 * qkv.size, transcendentals=work
        ),
        compiler_params=pltpu.CompilerParams(vmem_limit_bytes=40 << 20),
    )(qkv, qkv, qkv, doc_column, doc_row)


def attend_backward(qkv, grad_mixed, doc_column, doc_row, half):
    seqs = doc_row.shape[0]
    heads, docs = head_specs(half * PAIRS)
    work = seqs * H * SEQ_LEN * SEQ_LEN // 2
    return pl.pallas_call(
        attend_backward_kernel,
        grid=(seqs, PAIRS),
        out_shape=[
            jax.ShapeDtypeStruct((seqs * SEQ_LEN, 3 * HALF), jnp.bfloat16),
            jax.ShapeDtypeStruct((1, 3 * HALF), jnp.float32),
        ],
        in_specs=heads
        + [pl.BlockSpec((SEQ_LEN, 128), lambda seq, pair: (seq, half * PAIRS + pair))]
        + docs,
        out_specs=[
            pl.BlockSpec((SEQ_LEN, 3 * HALF), lambda seq, pair: (seq, 0)),
            pl.BlockSpec((1, 3 * HALF), lambda seq, pair: (0, 0)),
        ],
        cost_estimate=pl.CostEstimate(
            flops=40 * DH * work, bytes_accessed=8 * qkv.size, transcendentals=work
        ),
        compiler_params=pltpu.CompilerParams(vmem_limit_bytes=50 << 20),
    )(qkv, qkv, qkv, grad_mixed, doc_column, doc_row)


CHUNK = 512
TILE = 256


def part_out(core, values, parted, blocks):
    width = values.shape[1] // blocks
    for block in range(blocks):
        half = (block % 2 + core + 1) % 2
        start = block // 2 * width
        parted[half, :, start : start + width] = values[:, block * width : (block + 1) * width]


def load(plan, spot, pieces, whole, sem):
    copies = []
    for source, flip, out, rows, columns, start in plan:
        if flip is None:
            target = whole[out]
        else:
            x, c, y = ((spot[i] + flip[i]) % 2 for i in range(3))
            target = whole[out].at[x, c, :, y, :, pl.ds(columns[0], columns[1])]
        part = pieces[source] if flip is None else pieces[source].at[:, pl.ds(start, rows), :]
        copies.append(pltpu.make_async_copy(part, target, sem.at[len(copies)]))
    return copies


def fetch(plan, spot, pieces, whole, sem):
    @pl.when(pl.program_id(0) == 0)
    def _():
        copies = load(plan, spot, pieces, whole, sem)
        for copy in copies:
            copy.start()
        for copy in copies:
            copy.wait()


def columns_of(weight, start, size):
    return weight[..., start : start + size].reshape(-1, size)


def block_of(weight, block):
    return weight[block // CORES, block % CORES].reshape(-1, weight.shape[-1])


def middle_up_kernel(plan, blocks, count, spot, *refs):
    pieces, refs = refs[:count], refs[count:]
    mixed, tokens, vectors, bias_up = refs[:4]
    first_full, normed, scale, active_parts, slope, first_parts, mixed_parts, token_parts = refs[4:12]
    w_out, w_up, sem = refs[12:]
    fetch(plan, spot, pieces, (w_out, w_up), sem)
    core = spot[1]
    bias_out, gain_one, shift_one = (vectors[i : i + 1, :] for i in range(3))
    part_out(core, mixed[...], mixed_parts, blocks)
    part_out(core, tokens[...], token_parts, blocks)
    hidden = tokens[...].astype(jnp.float32) + matmul(mixed[...], columns_of(w_out, 0, D)) + bias_out
    normed_one, scale_one = norm_forward(hidden)
    normed[...] = normed_one
    scale[...] = jnp.broadcast_to(scale_one, scale.shape)
    first_out = normed_one * gain_one + shift_one
    first_full[...] = first_out
    first_low = first_out.astype(jnp.bfloat16)
    part_out(core, first_low, first_parts, blocks)
    wide = w_up.shape[-1]
    width = wide // blocks
    for start in range(0, wide, CHUNK):
        at = slice(start, start + CHUNK)
        upward = matmul(first_low, columns_of(w_up, start, CHUNK)) + bias_up[:, at]
        phi = 0.5 * (1.0 + lax.erf(upward * 0.7071067811865476))
        active = (upward * phi).astype(jnp.bfloat16)
        slope[:, at] = (
            phi + upward * jnp.exp(-0.5 * upward * upward) * 0.3989422804014327
        ).astype(jnp.bfloat16)
        block, inside = start // width, start % width
        half = (block % 2 + core + 1) % 2
        place = block // 2 * width + inside
        active_parts[half, :, place : place + CHUNK] = active


def middle_down_kernel(plan, blocks, count, spot, *refs):
    pieces, refs = refs[:count], refs[count:]
    first_full, active_parts, cotangent, vectors = refs[:4]
    output, grad_sum, grad_low, sums, w_down, sem = refs[4:]
    fetch(plan, spot, pieces, (w_down,), sem)
    bias_down, gain_two, shift_two = (vectors[i : i + 1, :] for i in range(3, 6))
    second = first_full[...] + bias_down
    width = active_parts.shape[2] * 2 // blocks
    for block in range(blocks):
        half = (block % 2 + spot[1] + 1) % 2
        place = block // 2 * width
        part = active_parts[half, :, place : place + width]
        second = second + matmul(part, block_of(w_down, block))
    normed_two, scale_two = norm_forward(second)
    output[...] = (normed_two * gain_two + shift_two).astype(jnp.bfloat16)
    grad = cotangent[...]
    grad_second = norm_backward(grad, normed_two, scale_two, gain_two)
    grad_sum[...] = grad_second
    rounded = grad_second.astype(jnp.bfloat16)
    grad_low[...] = rounded

    @pl.when(pl.program_id(0) == 0)
    def _():
        sums[...] = jnp.zeros_like(sums)

    sums[0:1, :] += jnp.sum(grad * normed_two, axis=0, keepdims=True)
    sums[1:2, :] += jnp.sum(grad, axis=0, keepdims=True)
    sums[2:3, :] += jnp.sum(rounded.astype(jnp.float32), axis=0, keepdims=True)


def middle_backward_kernel(plan, count, spot, *refs):
    pieces, refs = refs[:count], refs[count:]
    grad_low, grad_sum, slope, normed, scale, vectors = refs[:6]
    grad_up, grad_hidden, branch, grad_mixed, sums, sums_up = refs[6:12]
    w_out, w_up, w_down, sem = refs[12:]
    fetch(plan, spot, pieces, (w_out, w_up, w_down), sem)

    @pl.when(pl.program_id(0) == 0)
    def _():
        sums[...] = jnp.zeros_like(sums)
        sums_up[...] = jnp.zeros_like(sums_up)

    grad_first = grad_sum[...]
    low = grad_low[...]
    wide = w_up.shape[-1]
    width = wide // (w_down.shape[0] * w_down.shape[1])
    for start in range(0, wide, CHUNK):
        at = slice(start, start + CHUNK)
        rows = block_of(w_down, start // width)[start % width : start % width + CHUNK]
        part = (across(low, rows) * slope[:, at].astype(jnp.float32)).astype(jnp.bfloat16)
        grad_up[:, at] = part
        sums_up[:, at] += jnp.sum(part.astype(jnp.float32), axis=0, keepdims=True)
        grad_first = grad_first + across(part, columns_of(w_up, start, CHUNK))
    normed_one = normed[...]
    sums[0:1, :] += jnp.sum(grad_first * normed_one, axis=0, keepdims=True)
    sums[1:2, :] += jnp.sum(grad_first, axis=0, keepdims=True)
    hidden = norm_backward(grad_first, normed_one, scale[:, 0:1], vectors[1:2, :])
    grad_hidden[...] = hidden
    rounded = hidden.astype(jnp.bfloat16)
    branch[...] = rounded
    sums[2:3, :] += jnp.sum(rounded.astype(jnp.float32), axis=0, keepdims=True)
    grad_mixed[...] = across(rounded, columns_of(w_out, 0, D)).astype(jnp.bfloat16)


def tiled(columns):
    return pl.BlockSpec((TILE, columns), lambda i: (i, 0))


def parted(columns):
    return pl.BlockSpec((2, TILE, columns), lambda i: (0, i, 0))


def resident(shape):
    return pl.BlockSpec(shape, lambda i: (0,) * len(shape), pipeline_mode=pl.Buffered(1))


def middle_call(kernel, grid, spot, weights, tiles, fixed, outs, sums, flops, exps=0):
    arrays, plan, shapes = weights
    rows = tiles[0].shape[-2]
    lead = (grid.xs, CORES, grid.zs, grid.ys)

    def spec(shape):
        return parted(shape[2]) if len(shape) == 3 else tiled(shape[1])

    return pl.pallas_call(
        functools.partial(kernel, plan),
        grid=(rows // TILE,),
        out_shape=[jax.ShapeDtypeStruct(*o) for o in outs]
        + [jax.ShapeDtypeStruct(o, jnp.float32) for o in sums],
        in_specs=[pl.BlockSpec(memory_space=pltpu.SMEM)]
        + [pl.BlockSpec(memory_space=pl.ANY)] * len(arrays)
        + [spec(t.shape) for t in tiles]
        + [resident(f.shape) for f in fixed],
        out_specs=[spec(o[0]) for o in outs] + [pl.BlockSpec(o, lambda i: (0, 0)) for o in sums],
        scratch_shapes=[pltpu.VMEM(lead + shape, jnp.bfloat16) for shape in shapes]
        + [pltpu.SemaphoreType.DMA((len(plan),))],
        cost_estimate=pl.CostEstimate(flops=flops, bytes_accessed=40 << 20, transcendentals=exps),
        compiler_params=pltpu.CompilerParams(vmem_limit_bytes=60 << 20),
    )(spot, *arrays, *tiles, *fixed)


def joined(*weights):
    arrays, plan, shapes = [], [], []
    for some, steps, sizes in weights:
        for source, flip, out, rows, columns, start in steps:
            place = (source + len(arrays), flip, out + len(shapes), rows, columns, start)
            plan.append(place)
        arrays, shapes = arrays + list(some), shapes + list(sizes)
    return arrays, plan, shapes


def middle_up(grid, spot, weights, mixed, tokens, vectors, bias_up):
    rows, wide = tokens.shape[0], bias_up.shape[1]
    outs = [
        ((rows, D), jnp.float32),
        ((rows, D), jnp.float32),
        ((rows, 128), jnp.float32),
        ((2, rows, wide // 2), jnp.bfloat16),
        ((rows, wide), jnp.bfloat16),
        ((2, rows, D // 2), jnp.bfloat16),
        ((2, rows, D // 2), jnp.bfloat16),
        ((2, rows, D // 2), jnp.bfloat16),
    ]

    def kernel(plan, *refs):
        middle_up_kernel(plan, grid.xs * CORES, len(weights[0]), *refs)

    flops = 2 * rows * D * (D + wide)
    return middle_call(
        kernel, grid, spot, weights, [mixed, tokens], [vectors, bias_up], outs, [], flops, 2 * rows * wide
    )


def middle_down(grid, spot, weights, first_full, active_parts, cotangent, vectors):
    rows, wide = first_full.shape[0], active_parts.shape[2] * 2
    outs = [((rows, D), jnp.bfloat16), ((rows, D), jnp.float32), ((rows, D), jnp.bfloat16)]

    def kernel(plan, *refs):
        middle_down_kernel(plan, grid.xs * CORES, len(weights[0]), *refs)

    tiles = [first_full, active_parts, cotangent]
    flops = 2 * rows * D * wide
    return middle_call(kernel, grid, spot, weights, tiles, [vectors], outs, [(8, D)], flops)


def middle_backward(grid, spot, weights, grad_low, grad_sum, slope, normed, scale, vectors):
    rows, wide = slope.shape
    outs = [
        ((rows, wide), jnp.bfloat16),
        ((rows, D), jnp.float32),
        ((rows, D), jnp.bfloat16),
        ((rows, D), jnp.bfloat16),
    ]

    def kernel(plan, *refs):
        middle_backward_kernel(plan, len(weights[0]), *refs)

    tiles = [grad_low, grad_sum, slope, normed, scale]
    flops = 2 * rows * D * (D + 2 * wide)
    return middle_call(
        kernel, grid, spot, weights, tiles, [vectors], outs, [(8, D), (1, wide)], flops
    )


class Grid:
    def __init__(self, mesh):
        self.shape = dict(mesh.shape)
        self.xs = self.shape["dp"] // CORES
        self.ys = self.xs
        self.zs = self.shape["fsdp"] // self.ys
        self.sizes = {"x": self.xs, "c": CORES, "z": self.zs, "y": self.ys}
        self.count = self.shape["dp"] * self.shape["fsdp"]
        self.pairs = self.xs == 2 and self.ys == 2 and self.zs == 4

    def at(self):
        dp, fsdp = lax.axis_index("dp"), lax.axis_index("fsdp")
        return {"x": dp // CORES, "c": dp % CORES, "z": fsdp // self.ys, "y": fsdp % self.ys}

    def shifted(self, axis, step, wrap):
        hops = []
        for x in range(self.xs):
            for c in range(CORES):
                for z in range(self.zs):
                    for y in range(self.ys):
                        to = {"x": x, "c": c, "z": z, "y": y}
                        to[axis] += step
                        if wrap:
                            to[axis] %= self.sizes[axis]
                        elif not 0 <= to[axis] < self.sizes[axis]:
                            continue
                        hops.append((self.number(x, c, z, y), self.number(**to)))
        return hops

    def number(self, x, c, z, y):
        return ((x * CORES + c) * self.zs + z) * self.ys + y

    def swap(self, values, axis):
        return lax.ppermute(values, AXES, self.shifted(axis, 1, True))

    def along(self, values, axis, step):
        return lax.ppermute(values, AXES, self.shifted(axis, step, False))


def place_kernel(steps, count, spot, *refs):
    arrays, out, sem = refs[:count], refs[count], refs[count + 1]

    def each(act):
        for index, (source, select, target, valid) in enumerate(steps):
            def run(index=index, source=source, select=select, target=target):
                part = arrays[source] if select is None else arrays[source].at[select]
                act(pltpu.make_async_copy(part, out.at[target(spot)], sem.at[index]))

            if valid is None:
                run()
            else:
                pl.when(valid(spot))(run)

    each(lambda copy: copy.start())
    each(lambda copy: copy.wait())


def place(arrays, spot, steps, shape):
    size = 4 * sum(a.size for a in arrays)
    return pl.pallas_call(
        functools.partial(place_kernel, steps, len(arrays)),
        out_shape=jax.ShapeDtypeStruct(shape, jnp.bfloat16),
        in_specs=[pl.BlockSpec(memory_space=pltpu.SMEM)]
        + [pl.BlockSpec(memory_space=pl.ANY)] * len(arrays),
        out_specs=pl.BlockSpec(memory_space=pl.ANY),
        scratch_shapes=[pltpu.SemaphoreType.DMA((len(steps),))],
        cost_estimate=pl.CostEstimate(flops=0, bytes_accessed=size, transcendentals=0),
        compiler_params=pltpu.CompilerParams(vmem_limit_bytes=1 << 20),
    )(spot, *arrays)


def line_gather(grid, spot, shard):
    arrays = [shard]
    steps = [(0, None, lambda spot: spot[3], None)]
    up = low = shard
    for hop in range(1, grid.zs):
        up, low = grid.along(up, "z", 1), grid.along(low, "z", -1)
        arrays += [up, low]
        last = grid.zs - 1
        steps.append(
            (
                2 * hop - 1,
                None,
                lambda spot, hop=hop: jnp.maximum(spot[3] - hop, 0),
                lambda spot, hop=hop: spot[3] >= hop,
            )
        )
        steps.append(
            (
                2 * hop,
                None,
                lambda spot, hop=hop: jnp.minimum(spot[3] + hop, last),
                lambda spot, hop=hop: spot[3] + hop <= last,
            )
        )
    return place(arrays, spot, steps, (grid.zs,) + shard.shape)


def own_swaps(grid, block, first, second):
    return grid.swap(block, first), grid.swap(block, second)


def pair_gather(grid, block, swapped, first, second):
    near, far = swapped
    pieces = {(0, 0): block, (1, 0): near, (0, 1): far, (1, 1): grid.swap(near, second)}
    found = {}
    for (one, two), piece in pieces.items():
        flips = {first: one, second: two}
        found[(flips["x"], 0, flips["y"])] = piece
        found[(flips["x"], 1, flips["y"])] = grid.swap(piece, "c")
    return found


def block_plan(parts):
    plan, arrays = [], []
    for pieces, targets in parts:
        for flip, piece in pieces.items():
            for out, rows, columns, start in targets:
                plan.append((len(arrays), flip, out, rows, columns, start))
            arrays.append(piece)
    return arrays, plan


def assemble_kernel(plan, count, spot, *refs):
    copies = load(plan, spot, refs[:count], refs[count:-1], refs[-1])
    for copy in copies:
        copy.start()
    for copy in copies:
        copy.wait()


def assemble(grid, spot, parts, shape):
    arrays, plan = block_plan(parts)
    size = sum(2 * piece.size for piece in arrays)
    whole = pl.pallas_call(
        functools.partial(assemble_kernel, plan, len(arrays)),
        out_shape=jax.ShapeDtypeStruct((grid.xs, CORES, grid.zs, grid.ys) + shape, jnp.bfloat16),
        in_specs=[pl.BlockSpec(memory_space=pltpu.SMEM)]
        + [pl.BlockSpec(memory_space=pl.ANY)] * len(arrays),
        out_specs=pl.BlockSpec(memory_space=pl.ANY),
        scratch_shapes=[pltpu.SemaphoreType.DMA((len(plan),))],
        cost_estimate=pl.CostEstimate(flops=0, bytes_accessed=2 * size, transcendentals=0),
        compiler_params=pltpu.CompilerParams(vmem_limit_bytes=1 << 20),
    )(spot, *arrays)
    return whole.reshape(grid.count * shape[0], shape[1])


def take(values, index, axis):
    return lax.dynamic_index_in_dim(values, index, axis, keepdims=False)


def total(terms):
    result = terms[0].astype(jnp.float32)
    for term in terms[1:]:
        result = result + term.astype(jnp.float32)
    return result


class Chain:
    def __init__(self, grid, at, sent, kept):
        self.grid, self.at = grid, at
        got = grid.swap(sent, "c")
        shape = (grid.xs, grid.zs, grid.ys, -1, sent.shape[1])
        terms = [kept.reshape(shape), got.reshape(shape)]
        cut = sent.shape[1] // 256 * 128
        self.sides = [[t[..., :cut] for t in terms], [t[..., cut:] for t in terms]]

    def give(self, *ways):
        self.ways = ways
        sent = []
        for terms, (name, axis) in zip(self.sides, ways):
            values = total([take(term, 1 - self.at[name], axis) for term in terms])
            sent.append(values.astype(jnp.bfloat16))
        return tuple(sent)

    def first(self):
        return self.give(("x", 0), ("y", 2))

    def swap(self, sent):
        return tuple(self.grid.swap(values, way[0]) for values, way in zip(sent, self.ways))

    def get(self, received):
        self.sides = [
            [take(term, self.at[name], axis) for term in terms] + [values]
            for terms, (name, axis), values in zip(self.sides, self.ways, received)
        ]

    def second(self, received):
        self.get(received)
        return self.give(("y", 1), ("x", 0))

    def block(self, received):
        self.get(received)
        return jnp.concatenate([total(terms) for terms in self.sides], axis=-1).astype(jnp.bfloat16)


class Line:
    def __init__(self, grid, at, block):
        self.grid, self.at, self.block = grid, at, block

    def own(self, index):
        index = jnp.clip(index, 0, self.grid.zs - 1)
        return take(self.block, index, 0).astype(jnp.float32)

    def give(self, hop, received=None):
        size = self.grid.zs
        sums = [self.own(self.at["z"] + size - hop), self.own(self.at["z"] - size + hop)]
        if received is not None:
            sums = [own + more.astype(jnp.float32) for own, more in zip(sums, received)]
        return tuple(values.astype(jnp.bfloat16) for values in sums)

    def move(self, sent):
        return tuple(self.grid.along(values, "z", step) for values, step in zip(sent, (1, -1)))

    def end(self, received):
        return total([self.own(self.at["z"]), *received])

    def rest(self, received, hop):
        for step in range(hop, self.grid.zs):
            received = self.move(self.give(step, received))
        return self.end(received)


def by_halves(parts):
    return jnp.concatenate([p[:, i : i + HALF] for i in (0, HALF) for p in parts], axis=1)


def small_kernel(*refs):
    rows = []
    for ref in refs[:-1]:
        row = ref[...].astype(jnp.float32)
        if row.shape[1] < 128:
            row = jnp.concatenate([row, jnp.zeros((1, 128 - row.shape[1]), jnp.float32)], axis=1)
        rows.append(row)
    rows.append(jnp.zeros((refs[-1].shape[0] - len(rows), 128), jnp.float32))
    refs[-1][...] = jnp.concatenate(rows, axis=0).astype(jnp.bfloat16)


def pack_small(smalls, rows):
    return pl.pallas_call(
        small_kernel, out_shape=jax.ShapeDtypeStruct((rows, 128), jnp.bfloat16)
    )(*[small[None] for small in smalls])


def pack_first(spot, attn, small):
    steps = []
    for half in range(2):
        for part in range(3):
            start = (3 * half + part) * HALF
            steps.append(
                (
                    part,
                    (slice(None), pl.ds(half * HALF, HALF)),
                    lambda spot, start=start: (slice(None), pl.ds(start, HALF)),
                    None,
                )
            )
    steps.append((3, None, lambda spot: (slice(None), pl.ds(3 * D, 128)), None))
    return place([*attn, small], spot, steps, (attn[0].shape[0], 3 * D + 128))


def pack_rest(spot, w_out, w_up, w_down):
    rows, wide = w_up.shape
    steps = [(0, None, lambda spot: (pl.ds(0, rows), slice(None)), None)]
    for i in range(wide // D):
        steps.append(
            (
                1,
                (slice(None), pl.ds(i * D, D)),
                lambda spot, i=i: (pl.ds((i + 1) * rows, rows), slice(None)),
                None,
            )
        )
    start = rows + rows * wide // D
    steps.append((2, None, lambda spot: (pl.ds(start, w_down.shape[0]), slice(None)), None))
    return place([w_out, w_up, w_down], spot, steps, (start + w_down.shape[0], D))


class Gather:
    orders = (("y", "x"), ("x", "y"))

    def __init__(self, grid, line):
        self.grid = grid
        self.cut = line.shape[2] // 256 * 128
        self.columns = line.shape[2]
        self.sides = [line[:, :, : self.cut], line[:, :, self.cut :]]

    def start(self):
        self.swaps = [own_swaps(self.grid, v, *o) for v, o in zip(self.sides, self.orders)]

    def blocks(self):
        return [
            pair_gather(self.grid, v, swapped, *order)
            for v, swapped, order in zip(self.sides, self.swaps, self.orders)
        ]

    def parts(self, targets):
        spans = [(0, self.cut), (self.cut, self.columns - self.cut)]
        return [
            (
                pieces,
                [(out, rows, (first + span[0], span[1]), start) for out, rows, first, start in targets],
            )
            for pieces, span in zip(self.blocks(), spans)
        ]


def split_small(small, widths):
    return [
        small[:, i, :width].reshape(-1).astype(jnp.float32) for i, width in enumerate(widths)
    ]


def hold(later, *ready):
    return lax.optimization_barrier((later, *ready))


def halves(parts, right):
    return tuple(outer_sum(parts[i], right).astype(jnp.bfloat16) for i in range(2))


def plain_reduce(grid, parts, right):
    both = [outer_sum(parts[i], right).reshape(grid.xs, -1, right.shape[1]) for i in (1, 0)]
    whole = jnp.stack(both, axis=1).reshape(-1, right.shape[1])
    return lax.psum_scatter(whole, AXES, scatter_dimension=0, tiled=True)


def per_device(
    grid,
    tokens,
    segment_ids,
    w_query,
    b_query,
    w_key,
    w_value,
    b_value,
    w_out,
    b_out,
    ln1_gain,
    ln1_bias,
    w_up,
    b_up,
    w_down,
    b_down,
    ln2_gain,
    ln2_bias,
    out_cotangent,
):
    at = grid.at()
    rows, wide = w_up.shape
    lower = w_down.shape[0]
    smalls = (b_query, b_value, b_out, ln1_gain, ln1_bias, b_down, ln2_gain, ln2_bias, b_up)
    widths = [small.shape[0] for small in smalls]
    attn = (w_query, w_key, w_value)
    low_tokens = tokens
    places = [at[name] for name in "xcyz"]
    spot = jnp.stack(places).astype(jnp.int32)
    if grid.pairs:
        first = line_gather(grid, spot, pack_first(spot, attn, pack_small(smalls, rows)))
        rest = pack_rest(spot, w_out, w_up, w_down)
        rest, first = hold(rest, first)
        gather = Gather(grid, first)
        gather.start()
        whole = assemble(grid, spot, gather.parts([(0, rows, 0, 0)]), (rows, 3 * D + 128))
        full_qkv, small = whole[:, : 3 * D], whole[:, 3 * D :].reshape(grid.count, rows, 128)
        line = line_gather(grid, spot, rest)
        low_tokens, line = hold(tokens, line)
        split = rows + rows * wide // D
        up_gather, down_gather = Gather(grid, line[:, :split]), Gather(grid, line[:, split:])
        up_gather.start()
    else:
        full_qkv, full_out, full_up, full_down = (
            lax.all_gather(w, AXES, axis=0, tiled=True)
            for w in (by_halves(attn), w_out, w_up, w_down)
        )
        small = jnp.stack([jnp.pad(v, (0, max(widths) - v.shape[0])) for v in smalls])
        small = lax.all_gather(small[None], AXES, axis=0, tiled=True)
    bias_query, bias_value, *others, bias_up = split_small(small, widths)
    vectors = jnp.stack(others + [jnp.zeros_like(bias_query)] * 2)
    doc_row, doc_column = segment_ids[:, None, :], segment_ids[:, :, None]
    biases = (bias_query, jnp.zeros_like(bias_query), bias_value)
    bias_qkv = by_halves([bias[None] for bias in biases])
    qkv = (matmul(low_tokens, full_qkv) + bias_qkv).astype(jnp.bfloat16)
    mixed = attend_forward(qkv, doc_column, doc_row)
    up_shapes, down_shapes = [(rows, D), (rows, wide)], [(lower, D)]
    if grid.pairs:
        up_gather.swaps, mixed = hold(up_gather.swaps, mixed)
        targets = [(0, rows, 0, 0)]
        targets += [(1, rows, i * D, (i + 1) * rows) for i in range(wide // D)]
        up_weights = (*block_plan(up_gather.parts(targets)), up_shapes)
        down_gather.sides, up_weights[0][:] = hold(down_gather.sides, up_weights[0])
        down_gather.start()
    else:
        spot = spot * 0
        lead = (grid.xs, CORES, grid.zs, grid.ys)
        up_weights = (
            [full_out.reshape(lead + (rows, D)), full_up.reshape(lead + (rows, wide))],
            [(0, None, 0, rows, None, 0), (1, None, 1, rows, None, 0)],
            up_shapes,
        )
    bias_wide = bias_up.reshape(1, -1)
    (
        first_full,
        normed,
        scale,
        active_parts,
        slope,
        first_parts,
        mixed_parts,
        token_parts,
    ) = middle_up(grid, spot, up_weights, mixed, tokens, vectors, bias_wide)
    if grid.pairs:
        down_gather.swaps, first_full = hold(down_gather.swaps, first_full)
        down_parts = down_gather.parts([(0, lower, 0, 0)])
        down_weights = (*block_plan(down_parts), down_shapes)
    else:
        down_weights = ([full_down.reshape(lead + (lower, D))], [(0, None, 0, lower, None, 0)], down_shapes)
    output, grad_sum, grad_low, sums_two = middle_down(
        grid, spot, down_weights, first_full, active_parts, out_cotangent, vectors
    )
    if grid.pairs:
        down_chain = Chain(grid, at, *halves(active_parts, grad_low))
        grad_low, down_sent = hold(grad_low, down_chain.first())
    made = middle_backward(
        grid, spot, joined(up_weights, down_weights), grad_low, grad_sum, slope, normed, scale, vectors
    )
    grad_up, grad_hidden, branch, grad_mixed, sums_one, sums_up = made
    if grid.pairs:
        received, grad_up, branch, grad_mixed = hold(
            down_chain.swap(down_sent), grad_up, branch, grad_mixed
        )
        down_sent, grad_up = hold(down_chain.second(received), grad_up)
        up_chain = Chain(grid, at, *halves(first_parts, grad_up))
        up_sent, received = hold(up_chain.first(), down_chain.swap(down_sent))
        down_line = Line(grid, at, down_chain.block(received))
        down_sent, up_sent, grad_mixed = hold(down_line.give(1), up_sent, grad_mixed)
    one, sums_first = attend_backward(qkv, grad_mixed, doc_column, doc_row, 0)
    if grid.pairs:
        received, down_got, one, branch, grad_mixed = hold(
            up_chain.swap(up_sent), down_line.move(down_sent), one, branch, grad_mixed
        )
        up_sent, down_sent, one, branch = hold(
            up_chain.second(received), down_line.give(2, down_got), one, branch
        )
        of_qkv, of_out = halves(token_parts, one), halves(mixed_parts, branch)
        early = [jnp.concatenate([of_qkv[i], of_out[i]], axis=1) for i in range(2)]
        early_chain = Chain(grid, at, *early)
        early_sent, received, down_got = hold(
            early_chain.first(), up_chain.swap(up_sent), down_line.move(down_sent)
        )
        up_line = Line(grid, at, up_chain.block(received))
        up_sent, down_sent, early_sent, grad_mixed = hold(
            up_line.give(1), down_line.give(3, down_got), early_sent, grad_mixed
        )
    two, sums_second = attend_backward(qkv, grad_mixed, doc_column, doc_row, 1)
    if grid.pairs:
        received, up_got, down_got, two = hold(
            early_chain.swap(early_sent), up_line.move(up_sent), down_line.move(down_sent), two
        )
        early_sent, up_sent, two = hold(early_chain.second(received), up_line.give(2, up_got), two)
    sums_first, sums_second = sums_first[0], sums_second[0]
    totals = [
        jnp.concatenate([sums_first[:HALF], sums_second[:HALF]]),
        jnp.concatenate([sums_first[2 * HALF :], sums_second[2 * HALF :]]),
        sums_one[2],
        sums_one[0],
        sums_one[1],
        sums_up[0],
        sums_two[2],
        sums_two[0],
        sums_two[1],
    ]
    if grid.pairs:
        share_down = down_line.rest(down_got, grid.zs)
        packed = jnp.concatenate([v.reshape(grid.count, -1) for v in totals], axis=1)
        widths = [v.size // grid.count for v in totals]
        packed = jnp.pad(packed, ((0, 0), (0, rows * 128 - sum(widths)))).astype(jnp.bfloat16)
        packed = packed.reshape(grid.xs, CORES, -1, 128)
        ends = [take(packed, core_at, 1).reshape(-1, 128) for core_at in (1 - at["c"], at["c"])]
        of_qkv = halves(token_parts, two)
        late = [jnp.concatenate([of_qkv[i], ends[i]], axis=1) for i in range(2)]
        late_chain = Chain(grid, at, *late)
        late_sent, received, up_got = hold(
            late_chain.first(), early_chain.swap(early_sent), up_line.move(up_sent)
        )
        two, late_sent = hold(two, late_sent)
        share_up = up_line.rest(up_got, 3)
        early_block = early_chain.block(received)
        late_sent = late_chain.second(late_chain.swap(late_sent))
        late_block = late_chain.block(late_chain.swap(late_sent))
        line = Line(grid, at, jnp.concatenate([early_block, late_block], axis=2))
        block = line.rest(line.move(line.give(1)), 2)
        early, share_out = block[:, : 3 * HALF], block[:, 3 * HALF : 5 * HALF]
        late = block[:, 5 * HALF :]
        flat = late[:, 3 * HALF :].reshape(-1)
        shares, start = [], 0
        for width in widths:
            shares.append(flat[start : start + width])
            start += width
    else:
        share_down = plain_reduce(grid, active_parts, grad_low)
        share_up = plain_reduce(grid, first_parts, grad_up)
        share_out = plain_reduce(grid, mixed_parts, branch)
        early, late = plain_reduce(grid, token_parts, one), plain_reduce(grid, token_parts, two)
        shares = [lax.psum_scatter(v, AXES, scatter_dimension=0, tiled=True) for v in totals]
    share_query, share_key, share_value = (
        jnp.concatenate([part[:, i : i + HALF] for part in (early, late)], axis=1)
        for i in range(0, 3 * HALF, HALF)
    )
    tokens_grad = (
        grad_hidden
        + back_matmul(one, full_qkv[:, : 3 * HALF])
        + back_matmul(two, full_qkv[:, 3 * HALF :])
    ).astype(jnp.bfloat16)
    return (
        output,
        tokens_grad,
        share_query,
        shares[0],
        share_key,
        share_value,
        shares[1],
        share_out,
        *shares[2:5],
        share_up,
        shares[5],
        share_down,
        *shares[6:],
    )


def solution(mesh):
    rows, flat = P(AXES, None), P(AXES)
    in_specs = (rows,) * 3 + (flat, rows, rows, flat, rows, flat, flat, flat, rows, flat, rows)
    in_specs += (flat,) * 3 + (rows,)
    out_specs = (rows,) * 3 + (flat, rows, rows, flat, rows, flat, flat, flat, rows, flat, rows)
    out_specs += (flat,) * 3
    return jax.shard_map(
        functools.partial(per_device, Grid(mesh)),
        mesh=mesh,
        in_specs=in_specs,
        out_specs=out_specs,
        check_vma=False,
    )
```

```python
import functools

import jax
import jax.numpy as jnp
from jax import lax
from jax.experimental import pallas as pl
from jax.experimental.pallas import tpu as pltpu
from jax.sharding import PartitionSpec as P

D = 1024
H = 16
DH = 64
SEQ_LEN = 512
AXES = ("dp", "fsdp")
CORES = 2


def matmul(operand, other):
    return jnp.dot(operand, other, preferred_element_type=jnp.float32)


def back_matmul(operand, other):
    return lax.dot_general(
        operand, other, (((1,), (1,)), ((), ())), preferred_element_type=jnp.float32
    )


def outer_sum(operand, other):
    return lax.dot_general(
        operand, other, (((0,), (0,)), ((), ())), preferred_element_type=jnp.float32
    )


def column_sum(values):
    return jnp.sum(values.astype(jnp.float32), axis=0)


def norm_forward(hidden):
    centred = hidden - jnp.mean(hidden, axis=-1, keepdims=True)
    scale_row = lax.rsqrt(jnp.mean(centred * centred, axis=-1, keepdims=True) + 1e-12)
    return (centred * scale_row, scale_row)


def norm_backward(grad_out, normed, scale_row, scaling):
    scaled = grad_out * scaling
    return scale_row * (
        scaled
        - jnp.mean(scaled, axis=-1, keepdims=True)
        - normed * jnp.mean(scaled * normed, axis=-1, keepdims=True)
    )


def across(operand, other):
    return lax.dot_general(
        operand, other, (((1,), (1,)), ((), ())), preferred_element_type=jnp.float32
    )


def down(operand, other):
    return lax.dot_general(
        operand, other, (((0,), (0,)), ((), ())), preferred_element_type=jnp.float32
    )


def attend_forward_kernel(query, key, value, doc_column, doc_row, mixed):
    same = doc_column[0] == doc_row[0]
    heads = []
    for head in range(2):
        lanes = slice(head * DH, (head + 1) * DH)
        scores = across(key[:, lanes], query[:, lanes] * jnp.bfloat16(0.125))
        scores = jnp.where(same, scores, -1000000000.0)
        powers = jnp.exp(scores - jnp.max(scores, axis=0, keepdims=True))
        row_total = jnp.sum(powers, axis=0, keepdims=True)
        heads.append(down(value[:, lanes], powers.astype(jnp.bfloat16)) * (1.0 / row_total))
    mixed[...] = jnp.concatenate(heads, axis=0).T.astype(jnp.bfloat16)


def attend_backward_kernel(query, key, value, grad, doc_column, doc_row, out, sums):
    same = doc_column[0] == doc_row[0]
    step = pl.program_id(1)
    found = ([], [], [])
    for head in range(2):
        lanes = slice(head * DH, (head + 1) * DH)
        scaled = query[:, lanes] * jnp.bfloat16(0.125)
        scores = jnp.where(same, across(key[:, lanes], scaled), -1000000000.0)
        powers = jnp.exp(scores - jnp.max(scores, axis=0, keepdims=True))
        probability = powers * (1.0 / jnp.sum(powers, axis=0, keepdims=True))
        grad_prob = across(value[:, lanes], grad[:, lanes])
        delta = jnp.sum(probability * grad_prob, axis=0, keepdims=True)
        grad_scores = (probability * (grad_prob - delta)).astype(jnp.bfloat16)
        found[0].append(down(key[:, lanes], grad_scores) * 0.125)
        found[1].append(matmul(grad_scores, scaled))
        found[2].append(matmul(probability.astype(jnp.bfloat16), grad[:, lanes]))
    grads = (
        jnp.concatenate(found[0], axis=0).T,
        jnp.concatenate(found[1], axis=1),
        jnp.concatenate(found[2], axis=1),
    )
    first = pl.program_id(0) == 0
    for index, value_of in enumerate(grads):
        rounded = value_of.astype(jnp.bfloat16)
        place = pl.ds(pl.multiple_of(index * HALF + step * 128, 128), 128)
        out[:, place] = rounded
        if index != 1:
            more = jnp.sum(rounded.astype(jnp.float32), axis=0, keepdims=True)
            sums[:, place] = jnp.where(first, 0.0, sums[:, place]) + more


HALF = D // 2
PAIRS = HALF // 128


def head_specs(start):
    def block(part):
        def index(seq, pair):
            pair = pair + start
            return seq, pair // PAIRS * (3 * PAIRS) + part * PAIRS + pair % PAIRS

        return pl.BlockSpec((SEQ_LEN, 128), index)

    docs = [
        pl.BlockSpec((1, SEQ_LEN, 1), lambda seq, pair: (seq, 0, 0)),
        pl.BlockSpec((1, 1, SEQ_LEN), lambda seq, pair: (seq, 0, 0)),
    ]
    return [block(i) for i in range(3)], docs


def attend_forward(qkv, doc_column, doc_row):
    seqs = doc_row.shape[0]
    heads, docs = head_specs(0)
    work = seqs * H * SEQ_LEN * SEQ_LEN
    return pl.pallas_call(
        attend_forward_kernel,
        grid=(seqs, 2 * PAIRS),
        out_shape=jax.ShapeDtypeStruct((seqs * SEQ_LEN, D), jnp.bfloat16),
        in_specs=heads + docs,
        out_specs=pl.BlockSpec((SEQ_LEN, 128), lambda seq, pair: (seq, pair)),
        cost_estimate=pl.CostEstimate(
            flops=16 * DH * work, bytes_accessed=8 * qkv.size, transcendentals=work
        ),
        compiler_params=pltpu.CompilerParams(vmem_limit_bytes=40 << 20),
    )(qkv, qkv, qkv, doc_column, doc_row)


def attend_backward(qkv, grad_mixed, doc_column, doc_row, half):
    seqs = doc_row.shape[0]
    heads, docs = head_specs(half * PAIRS)
    work = seqs * H * SEQ_LEN * SEQ_LEN // 2
    return pl.pallas_call(
        attend_backward_kernel,
        grid=(seqs, PAIRS),
        out_shape=[
            jax.ShapeDtypeStruct((seqs * SEQ_LEN, 3 * HALF), jnp.bfloat16),
            jax.ShapeDtypeStruct((1, 3 * HALF), jnp.float32),
        ],
        in_specs=heads
        + [pl.BlockSpec((SEQ_LEN, 128), lambda seq, pair: (seq, half * PAIRS + pair))]
        + docs,
        out_specs=[
            pl.BlockSpec((SEQ_LEN, 3 * HALF), lambda seq, pair: (seq, 0)),
            pl.BlockSpec((1, 3 * HALF), lambda seq, pair: (0, 0)),
        ],
        cost_estimate=pl.CostEstimate(
            flops=40 * DH * work, bytes_accessed=8 * qkv.size, transcendentals=work
        ),
        compiler_params=pltpu.CompilerParams(vmem_limit_bytes=50 << 20),
    )(qkv, qkv, qkv, grad_mixed, doc_column, doc_row)


CHUNK = 512
TILE = 256


def part_out(core, values, parted, blocks):
    width = values.shape[1] // blocks
    for block in range(blocks):
        half = (block % 2 + core + 1) % 2
        start = block // 2 * width
        parted[half, :, start : start + width] = values[:, block * width : (block + 1) * width]


def load(plan, spot, pieces, whole, sem):
    copies = []
    for source, flip, out, rows, columns, start in plan:
        if flip is None:
            target = whole[out]
        else:
            x, c, y = ((spot[i] + flip[i]) % 2 for i in range(3))
            target = whole[out].at[x, c, :, y, :, pl.ds(columns[0], columns[1])]
        part = pieces[source] if flip is None else pieces[source].at[:, pl.ds(start, rows), :]
        copies.append(pltpu.make_async_copy(part, target, sem.at[len(copies)]))
    return copies


def fetch(plan, spot, pieces, whole, sem):
    @pl.when(pl.program_id(0) == 0)
    def _():
        copies = load(plan, spot, pieces, whole, sem)
        for copy in copies:
            copy.start()
        for copy in copies:
            copy.wait()


def columns_of(weight, start, size):
    return weight[..., start : start + size].reshape(-1, size)


def block_of(weight, block):
    return weight[block // CORES, block % CORES].reshape(-1, weight.shape[-1])


def middle_up_kernel(plan, blocks, count, spot, *refs):
    pieces, refs = refs[:count], refs[count:]
    mixed, tokens, vectors, bias_up = refs[:4]
    first_full, normed, scale, active_parts, slope, first_parts, mixed_parts, token_parts = refs[4:12]
    w_out, w_up, sem = refs[12:]
    fetch(plan, spot, pieces, (w_out, w_up), sem)
    core = spot[1]
    bias_out, gain_one, shift_one = (vectors[i : i + 1, :] for i in range(3))
    part_out(core, mixed[...], mixed_parts, blocks)
    part_out(core, tokens[...], token_parts, blocks)
    hidden = tokens[...].astype(jnp.float32) + matmul(mixed[...], columns_of(w_out, 0, D)) + bias_out
    normed_one, scale_one = norm_forward(hidden)
    normed[...] = normed_one
    scale[...] = jnp.broadcast_to(scale_one, scale.shape)
    first_out = normed_one * gain_one + shift_one
    first_full[...] = first_out
    first_low = first_out.astype(jnp.bfloat16)
    part_out(core, first_low, first_parts, blocks)
    wide = w_up.shape[-1]
    width = wide // blocks
    for start in range(0, wide, CHUNK):
        at = slice(start, start + CHUNK)
        upward = matmul(first_low, columns_of(w_up, start, CHUNK)) + bias_up[:, at]
        phi = 0.5 * (1.0 + lax.erf(upward * 0.7071067811865476))
        active = (upward * phi).astype(jnp.bfloat16)
        slope[:, at] = (
            phi + upward * jnp.exp(-0.5 * upward * upward) * 0.3989422804014327
        ).astype(jnp.bfloat16)
        block, inside = start // width, start % width
        half = (block % 2 + core + 1) % 2
        place = block // 2 * width + inside
        active_parts[half, :, place : place + CHUNK] = active


def middle_down_kernel(plan, blocks, count, spot, *refs):
    pieces, refs = refs[:count], refs[count:]
    first_full, active_parts, cotangent, vectors = refs[:4]
    output, grad_sum, grad_low, sums, w_down, sem = refs[4:]
    fetch(plan, spot, pieces, (w_down,), sem)
    bias_down, gain_two, shift_two = (vectors[i : i + 1, :] for i in range(3, 6))
    second = first_full[...] + bias_down
    width = active_parts.shape[2] * 2 // blocks
    for block in range(blocks):
        half = (block % 2 + spot[1] + 1) % 2
        place = block // 2 * width
        part = active_parts[half, :, place : place + width]
        second = second + matmul(part, block_of(w_down, block))
    normed_two, scale_two = norm_forward(second)
    output[...] = (normed_two * gain_two + shift_two).astype(jnp.bfloat16)
    grad = cotangent[...]
    grad_second = norm_backward(grad, normed_two, scale_two, gain_two)
    grad_sum[...] = grad_second
    rounded = grad_second.astype(jnp.bfloat16)
    grad_low[...] = rounded

    @pl.when(pl.program_id(0) == 0)
    def _():
        sums[...] = jnp.zeros_like(sums)

    sums[0:1, :] += jnp.sum(grad * normed_two, axis=0, keepdims=True)
    sums[1:2, :] += jnp.sum(grad, axis=0, keepdims=True)
    sums[2:3, :] += jnp.sum(rounded.astype(jnp.float32), axis=0, keepdims=True)


def middle_backward_kernel(plan, count, spot, *refs):
    pieces, refs = refs[:count], refs[count:]
    grad_low, grad_sum, slope, normed, scale, vectors = refs[:6]
    grad_up, grad_hidden, branch, grad_mixed, sums, sums_up = refs[6:12]
    w_out, w_up, w_down, sem = refs[12:]
    fetch(plan, spot, pieces, (w_out, w_up, w_down), sem)

    @pl.when(pl.program_id(0) == 0)
    def _():
        sums[...] = jnp.zeros_like(sums)
        sums_up[...] = jnp.zeros_like(sums_up)

    grad_first = grad_sum[...]
    low = grad_low[...]
    wide = w_up.shape[-1]
    width = wide // (w_down.shape[0] * w_down.shape[1])
    for start in range(0, wide, CHUNK):
        at = slice(start, start + CHUNK)
        rows = block_of(w_down, start // width)[start % width : start % width + CHUNK]
        part = (across(low, rows) * slope[:, at].astype(jnp.float32)).astype(jnp.bfloat16)
        grad_up[:, at] = part
        sums_up[:, at] += jnp.sum(part.astype(jnp.float32), axis=0, keepdims=True)
        grad_first = grad_first + across(part, columns_of(w_up, start, CHUNK))
    normed_one = normed[...]
    sums[0:1, :] += jnp.sum(grad_first * normed_one, axis=0, keepdims=True)
    sums[1:2, :] += jnp.sum(grad_first, axis=0, keepdims=True)
    hidden = norm_backward(grad_first, normed_one, scale[:, 0:1], vectors[1:2, :])
    grad_hidden[...] = hidden
    rounded = hidden.astype(jnp.bfloat16)
    branch[...] = rounded
    sums[2:3, :] += jnp.sum(rounded.astype(jnp.float32), axis=0, keepdims=True)
    grad_mixed[...] = across(rounded, columns_of(w_out, 0, D)).astype(jnp.bfloat16)


def tiled(columns):
    return pl.BlockSpec((TILE, columns), lambda i: (i, 0))


def parted(columns):
    return pl.BlockSpec((2, TILE, columns), lambda i: (0, i, 0))


def resident(shape):
    return pl.BlockSpec(shape, lambda i: (0,) * len(shape), pipeline_mode=pl.Buffered(1))


def middle_call(kernel, grid, spot, weights, tiles, fixed, outs, sums, flops, exps=0):
    arrays, plan, shapes = weights
    rows = tiles[0].shape[-2]
    lead = (grid.xs, CORES, grid.zs, grid.ys)

    def spec(shape):
        return parted(shape[2]) if len(shape) == 3 else tiled(shape[1])

    return pl.pallas_call(
        functools.partial(kernel, plan),
        grid=(rows // TILE,),
        out_shape=[jax.ShapeDtypeStruct(*o) for o in outs]
        + [jax.ShapeDtypeStruct(o, jnp.float32) for o in sums],
        in_specs=[pl.BlockSpec(memory_space=pltpu.SMEM)]
        + [pl.BlockSpec(memory_space=pl.ANY)] * len(arrays)
        + [spec(t.shape) for t in tiles]
        + [resident(f.shape) for f in fixed],
        out_specs=[spec(o[0]) for o in outs] + [pl.BlockSpec(o, lambda i: (0, 0)) for o in sums],
        scratch_shapes=[pltpu.VMEM(lead + shape, jnp.bfloat16) for shape in shapes]
        + [pltpu.SemaphoreType.DMA((len(plan),))],
        cost_estimate=pl.CostEstimate(flops=flops, bytes_accessed=40 << 20, transcendentals=exps),
        compiler_params=pltpu.CompilerParams(vmem_limit_bytes=60 << 20),
    )(spot, *arrays, *tiles, *fixed)


def joined(*weights):
    arrays, plan, shapes = [], [], []
    for some, steps, sizes in weights:
        for source, flip, out, rows, columns, start in steps:
            place = (source + len(arrays), flip, out + len(shapes), rows, columns, start)
            plan.append(place)
        arrays, shapes = arrays + list(some), shapes + list(sizes)
    return arrays, plan, shapes


def middle_up(grid, spot, weights, mixed, tokens, vectors, bias_up):
    rows, wide = tokens.shape[0], bias_up.shape[1]
    outs = [
        ((rows, D), jnp.float32),
        ((rows, D), jnp.float32),
        ((rows, 128), jnp.float32),
        ((2, rows, wide // 2), jnp.bfloat16),
        ((rows, wide), jnp.bfloat16),
        ((2, rows, D // 2), jnp.bfloat16),
        ((2, rows, D // 2), jnp.bfloat16),
        ((2, rows, D // 2), jnp.bfloat16),
    ]

    def kernel(plan, *refs):
        middle_up_kernel(plan, grid.xs * CORES, len(weights[0]), *refs)

    flops = 2 * rows * D * (D + wide)
    return middle_call(
        kernel, grid, spot, weights, [mixed, tokens], [vectors, bias_up], outs, [], flops, 2 * rows * wide
    )


def middle_down(grid, spot, weights, first_full, active_parts, cotangent, vectors):
    rows, wide = first_full.shape[0], active_parts.shape[2] * 2
    outs = [((rows, D), jnp.bfloat16), ((rows, D), jnp.float32), ((rows, D), jnp.bfloat16)]

    def kernel(plan, *refs):
        middle_down_kernel(plan, grid.xs * CORES, len(weights[0]), *refs)

    tiles = [first_full, active_parts, cotangent]
    flops = 2 * rows * D * wide
    return middle_call(kernel, grid, spot, weights, tiles, [vectors], outs, [(8, D)], flops)


def middle_backward(grid, spot, weights, grad_low, grad_sum, slope, normed, scale, vectors):
    rows, wide = slope.shape
    outs = [
        ((rows, wide), jnp.bfloat16),
        ((rows, D), jnp.float32),
        ((rows, D), jnp.bfloat16),
        ((rows, D), jnp.bfloat16),
    ]

    def kernel(plan, *refs):
        middle_backward_kernel(plan, len(weights[0]), *refs)

    tiles = [grad_low, grad_sum, slope, normed, scale]
    flops = 2 * rows * D * (D + 2 * wide)
    return middle_call(
        kernel, grid, spot, weights, tiles, [vectors], outs, [(8, D), (1, wide)], flops
    )


class Grid:
    def __init__(self, mesh):
        self.shape = dict(mesh.shape)
        self.xs = self.shape["dp"] // CORES
        self.ys = self.xs
        self.zs = self.shape["fsdp"] // self.ys
        self.sizes = {"x": self.xs, "c": CORES, "z": self.zs, "y": self.ys}
        self.count = self.shape["dp"] * self.shape["fsdp"]
        self.pairs = self.xs == 2 and self.ys == 2 and self.zs == 4

    def at(self):
        dp, fsdp = lax.axis_index("dp"), lax.axis_index("fsdp")
        return {"x": dp // CORES, "c": dp % CORES, "z": fsdp // self.ys, "y": fsdp % self.ys}

    def shifted(self, axis, step, wrap):
        hops = []
        for x in range(self.xs):
            for c in range(CORES):
                for z in range(self.zs):
                    for y in range(self.ys):
                        to = {"x": x, "c": c, "z": z, "y": y}
                        to[axis] += step
                        if wrap:
                            to[axis] %= self.sizes[axis]
                        elif not 0 <= to[axis] < self.sizes[axis]:
                            continue
                        hops.append((self.number(x, c, z, y), self.number(**to)))
        return hops

    def number(self, x, c, z, y):
        return ((x * CORES + c) * self.zs + z) * self.ys + y

    def swap(self, values, axis):
        return lax.ppermute(values, AXES, self.shifted(axis, 1, True))

    def along(self, values, axis, step):
        return lax.ppermute(values, AXES, self.shifted(axis, step, False))


def place_kernel(steps, count, spot, *refs):
    arrays, out, sem = refs[:count], refs[count], refs[count + 1]

    def each(act):
        for index, (source, select, target, valid) in enumerate(steps):
            def run(index=index, source=source, select=select, target=target):
                part = arrays[source] if select is None else arrays[source].at[select]
                act(pltpu.make_async_copy(part, out.at[target(spot)], sem.at[index]))

            if valid is None:
                run()
            else:
                pl.when(valid(spot))(run)

    each(lambda copy: copy.start())
    each(lambda copy: copy.wait())


def place(arrays, spot, steps, shape):
    size = 4 * sum(a.size for a in arrays)
    return pl.pallas_call(
        functools.partial(place_kernel, steps, len(arrays)),
        out_shape=jax.ShapeDtypeStruct(shape, jnp.bfloat16),
        in_specs=[pl.BlockSpec(memory_space=pltpu.SMEM)]
        + [pl.BlockSpec(memory_space=pl.ANY)] * len(arrays),
        out_specs=pl.BlockSpec(memory_space=pl.ANY),
        scratch_shapes=[pltpu.SemaphoreType.DMA((len(steps),))],
        cost_estimate=pl.CostEstimate(flops=0, bytes_accessed=size, transcendentals=0),
        compiler_params=pltpu.CompilerParams(vmem_limit_bytes=1 << 20),
    )(spot, *arrays)


def line_gather(grid, spot, shard):
    arrays = [shard]
    steps = [(0, None, lambda spot: spot[3], None)]
    up = low = shard
    for hop in range(1, grid.zs):
        up, low = grid.along(up, "z", 1), grid.along(low, "z", -1)
        arrays += [up, low]
        last = grid.zs - 1
        steps.append(
            (
                2 * hop - 1,
                None,
                lambda spot, hop=hop: jnp.maximum(spot[3] - hop, 0),
                lambda spot, hop=hop: spot[3] >= hop,
            )
        )
        steps.append(
            (
                2 * hop,
                None,
                lambda spot, hop=hop: jnp.minimum(spot[3] + hop, last),
                lambda spot, hop=hop: spot[3] + hop <= last,
            )
        )
    return place(arrays, spot, steps, (grid.zs,) + shard.shape)


def own_swaps(grid, block, first, second):
    return grid.swap(block, first), grid.swap(block, second)


def pair_gather(grid, block, swapped, first, second):
    near, far = swapped
    pieces = {(0, 0): block, (1, 0): near, (0, 1): far, (1, 1): grid.swap(near, second)}
    found = {}
    for (one, two), piece in pieces.items():
        flips = {first: one, second: two}
        found[(flips["x"], 0, flips["y"])] = piece
        found[(flips["x"], 1, flips["y"])] = grid.swap(piece, "c")
    return found


def block_plan(parts):
    plan, arrays = [], []
    for pieces, targets in parts:
        for flip, piece in pieces.items():
            for out, rows, columns, start in targets:
                plan.append((len(arrays), flip, out, rows, columns, start))
            arrays.append(piece)
    return arrays, plan


def assemble_kernel(plan, count, spot, *refs):
    copies = load(plan, spot, refs[:count], refs[count:-1], refs[-1])
    for copy in copies:
        copy.start()
    for copy in copies:
        copy.wait()


def assemble(grid, spot, parts, shape):
    arrays, plan = block_plan(parts)
    size = sum(2 * piece.size for piece in arrays)
    whole = pl.pallas_call(
        functools.partial(assemble_kernel, plan, len(arrays)),
        out_shape=jax.ShapeDtypeStruct((grid.xs, CORES, grid.zs, grid.ys) + shape, jnp.bfloat16),
        in_specs=[pl.BlockSpec(memory_space=pltpu.SMEM)]
        + [pl.BlockSpec(memory_space=pl.ANY)] * len(arrays),
        out_specs=pl.BlockSpec(memory_space=pl.ANY),
        scratch_shapes=[pltpu.SemaphoreType.DMA((len(plan),))],
        cost_estimate=pl.CostEstimate(flops=0, bytes_accessed=2 * size, transcendentals=0),
        compiler_params=pltpu.CompilerParams(vmem_limit_bytes=1 << 20),
    )(spot, *arrays)
    return whole.reshape(grid.count * shape[0], shape[1])


def take(values, index, axis):
    return lax.dynamic_index_in_dim(values, index, axis, keepdims=False)


def total(terms):
    result = terms[0].astype(jnp.float32)
    for term in terms[1:]:
        result = result + term.astype(jnp.float32)
    return result


class Chain:
    def __init__(self, grid, at, sent, kept):
        self.grid, self.at = grid, at
        got = grid.swap(sent, "c")
        shape = (grid.xs, grid.zs, grid.ys, -1, sent.shape[1])
        terms = [kept.reshape(shape), got.reshape(shape)]
        cut = sent.shape[1] // 256 * 128
        self.sides = [[t[..., :cut] for t in terms], [t[..., cut:] for t in terms]]

    def give(self, *ways):
        self.ways = ways
        sent = []
        for terms, (name, axis) in zip(self.sides, ways):
            values = total([take(term, 1 - self.at[name], axis) for term in terms])
            sent.append(values.astype(jnp.bfloat16))
        return tuple(sent)

    def first(self):
        return self.give(("x", 0), ("y", 2))

    def swap(self, sent):
        return tuple(self.grid.swap(values, way[0]) for values, way in zip(sent, self.ways))

    def get(self, received):
        self.sides = [
            [take(term, self.at[name], axis) for term in terms] + [values]
            for terms, (name, axis), values in zip(self.sides, self.ways, received)
        ]

    def second(self, received):
        self.get(received)
        return self.give(("y", 1), ("x", 0))

    def block(self, received):
        self.get(received)
        return jnp.concatenate([total(terms) for terms in self.sides], axis=-1).astype(jnp.bfloat16)


class Line:
    def __init__(self, grid, at, block):
        self.grid, self.at, self.block = grid, at, block

    def own(self, index):
        index = jnp.clip(index, 0, self.grid.zs - 1)
        return take(self.block, index, 0).astype(jnp.float32)

    def give(self, hop, received=None):
        size = self.grid.zs
        sums = [self.own(self.at["z"] + size - hop), self.own(self.at["z"] - size + hop)]
        if received is not None:
            sums = [own + more.astype(jnp.float32) for own, more in zip(sums, received)]
        return tuple(values.astype(jnp.bfloat16) for values in sums)

    def move(self, sent):
        return tuple(self.grid.along(values, "z", step) for values, step in zip(sent, (1, -1)))

    def end(self, received):
        return total([self.own(self.at["z"]), *received])

    def rest(self, received, hop):
        for step in range(hop, self.grid.zs):
            received = self.move(self.give(step, received))
        return self.end(received)


def by_halves(parts):
    return jnp.concatenate([p[:, i : i + HALF] for i in (0, HALF) for p in parts], axis=1)


def small_kernel(*refs):
    rows = []
    for ref in refs[:-1]:
        row = ref[...].astype(jnp.float32)
        if row.shape[1] < 128:
            row = jnp.concatenate([row, jnp.zeros((1, 128 - row.shape[1]), jnp.float32)], axis=1)
        rows.append(row)
    rows.append(jnp.zeros((refs[-1].shape[0] - len(rows), 128), jnp.float32))
    refs[-1][...] = jnp.concatenate(rows, axis=0).astype(jnp.bfloat16)


def pack_small(smalls, rows):
    return pl.pallas_call(
        small_kernel, out_shape=jax.ShapeDtypeStruct((rows, 128), jnp.bfloat16)
    )(*[small[None] for small in smalls])


def pack_first(spot, attn, small):
    steps = []
    for half in range(2):
        for part in range(3):
            start = (3 * half + part) * HALF
            steps.append(
                (
                    part,
                    (slice(None), pl.ds(half * HALF, HALF)),
                    lambda spot, start=start: (slice(None), pl.ds(start, HALF)),
                    None,
                )
            )
    steps.append((3, None, lambda spot: (slice(None), pl.ds(3 * D, 128)), None))
    return place([*attn, small], spot, steps, (attn[0].shape[0], 3 * D + 128))


def pack_rest(spot, w_out, w_up, w_down):
    rows, wide = w_up.shape
    steps = [(0, None, lambda spot: (pl.ds(0, rows), slice(None)), None)]
    for i in range(wide // D):
        steps.append(
            (
                1,
                (slice(None), pl.ds(i * D, D)),
                lambda spot, i=i: (pl.ds((i + 1) * rows, rows), slice(None)),
                None,
            )
        )
    start = rows + rows * wide // D
    steps.append((2, None, lambda spot: (pl.ds(start, w_down.shape[0]), slice(None)), None))
    return place([w_out, w_up, w_down], spot, steps, (start + w_down.shape[0], D))


class Gather:
    orders = (("y", "x"), ("x", "y"))

    def __init__(self, grid, line):
        self.grid = grid
        self.cut = line.shape[2] // 256 * 128
        self.columns = line.shape[2]
        self.sides = [line[:, :, : self.cut], line[:, :, self.cut :]]

    def start(self):
        self.swaps = [own_swaps(self.grid, v, *o) for v, o in zip(self.sides, self.orders)]

    def blocks(self):
        return [
            pair_gather(self.grid, v, swapped, *order)
            for v, swapped, order in zip(self.sides, self.swaps, self.orders)
        ]

    def parts(self, targets):
        spans = [(0, self.cut), (self.cut, self.columns - self.cut)]
        return [
            (
                pieces,
                [(out, rows, (first + span[0], span[1]), start) for out, rows, first, start in targets],
            )
            for pieces, span in zip(self.blocks(), spans)
        ]


def split_small(small, widths):
    return [
        small[:, i, :width].reshape(-1).astype(jnp.float32) for i, width in enumerate(widths)
    ]


def hold(later, *ready):
    return lax.optimization_barrier((later, *ready))


def halves(parts, right):
    return tuple(outer_sum(parts[i], right).astype(jnp.bfloat16) for i in range(2))


def plain_reduce(grid, parts, right):
    both = [outer_sum(parts[i], right).reshape(grid.xs, -1, right.shape[1]) for i in (1, 0)]
    whole = jnp.stack(both, axis=1).reshape(-1, right.shape[1])
    return lax.psum_scatter(whole, AXES, scatter_dimension=0, tiled=True)


def per_device(
    grid,
    tokens,
    segment_ids,
    w_query,
    b_query,
    w_key,
    w_value,
    b_value,
    w_out,
    b_out,
    ln1_gain,
    ln1_bias,
    w_up,
    b_up,
    w_down,
    b_down,
    ln2_gain,
    ln2_bias,
    out_cotangent,
):
    at = grid.at()
    rows, wide = w_up.shape
    lower = w_down.shape[0]
    smalls = (b_query, b_value, b_out, ln1_gain, ln1_bias, b_down, ln2_gain, ln2_bias, b_up)
    widths = [small.shape[0] for small in smalls]
    attn = (w_query, w_key, w_value)
    low_tokens = tokens
    places = [at[name] for name in "xcyz"]
    spot = jnp.stack(places).astype(jnp.int32)
    if grid.pairs:
        first = line_gather(grid, spot, pack_first(spot, attn, pack_small(smalls, rows)))
        rest = pack_rest(spot, w_out, w_up, w_down)
        rest, first = hold(rest, first)
        gather = Gather(grid, first)
        gather.start()
        whole = assemble(grid, spot, gather.parts([(0, rows, 0, 0)]), (rows, 3 * D + 128))
        full_qkv, small = whole[:, : 3 * D], whole[:, 3 * D :].reshape(grid.count, rows, 128)
        line = line_gather(grid, spot, rest)
        low_tokens, line = hold(tokens, line)
        split = rows + rows * wide // D
        up_gather, down_gather = Gather(grid, line[:, :split]), Gather(grid, line[:, split:])
        up_gather.start()
    else:
        full_qkv, full_out, full_up, full_down = (
            lax.all_gather(w, AXES, axis=0, tiled=True)
            for w in (by_halves(attn), w_out, w_up, w_down)
        )
        small = jnp.stack([jnp.pad(v, (0, max(widths) - v.shape[0])) for v in smalls])
        small = lax.all_gather(small[None], AXES, axis=0, tiled=True)
    bias_query, bias_value, *others, bias_up = split_small(small, widths)
    vectors = jnp.stack(others + [jnp.zeros_like(bias_query)] * 2)
    doc_row, doc_column = segment_ids[:, None, :], segment_ids[:, :, None]
    biases = (bias_query, jnp.zeros_like(bias_query), bias_value)
    bias_qkv = by_halves([bias[None] for bias in biases])
    qkv = (matmul(low_tokens, full_qkv) + bias_qkv).astype(jnp.bfloat16)
    mixed = attend_forward(qkv, doc_column, doc_row)
    up_shapes, down_shapes = [(rows, D), (rows, wide)], [(lower, D)]
    if grid.pairs:
        up_gather.swaps, mixed = hold(up_gather.swaps, mixed)
        targets = [(0, rows, 0, 0)]
        targets += [(1, rows, i * D, (i + 1) * rows) for i in range(wide // D)]
        up_weights = (*block_plan(up_gather.parts(targets)), up_shapes)
        down_gather.sides, up_weights[0][:] = hold(down_gather.sides, up_weights[0])
        down_gather.start()
    else:
        spot = spot * 0
        lead = (grid.xs, CORES, grid.zs, grid.ys)
        up_weights = (
            [full_out.reshape(lead + (rows, D)), full_up.reshape(lead + (rows, wide))],
            [(0, None, 0, rows, None, 0), (1, None, 1, rows, None, 0)],
            up_shapes,
        )
    bias_wide = bias_up.reshape(1, -1)
    (
        first_full,
        normed,
        scale,
        active_parts,
        slope,
        first_parts,
        mixed_parts,
        token_parts,
    ) = middle_up(grid, spot, up_weights, mixed, tokens, vectors, bias_wide)
    if grid.pairs:
        down_gather.swaps, first_full = hold(down_gather.swaps, first_full)
        down_parts = down_gather.parts([(0, lower, 0, 0)])
        down_weights = (*block_plan(down_parts), down_shapes)
    else:
        down_weights = ([full_down.reshape(lead + (lower, D))], [(0, None, 0, lower, None, 0)], down_shapes)
    output, grad_sum, grad_low, sums_two = middle_down(
        grid, spot, down_weights, first_full, active_parts, out_cotangent, vectors
    )
    if grid.pairs:
        down_chain = Chain(grid, at, *halves(active_parts, grad_low))
        grad_low, down_sent = hold(grad_low, down_chain.first())
    made = middle_backward(
        grid, spot, joined(up_weights, down_weights), grad_low, grad_sum, slope, normed, scale, vectors
    )
    grad_up, grad_hidden, branch, grad_mixed, sums_one, sums_up = made
    if grid.pairs:
        received, grad_up, branch, grad_mixed = hold(
            down_chain.swap(down_sent), grad_up, branch, grad_mixed
        )
        down_sent, grad_up = hold(down_chain.second(received), grad_up)
        up_chain = Chain(grid, at, *halves(first_parts, grad_up))
        up_sent, received = hold(up_chain.first(), down_chain.swap(down_sent))
        down_line = Line(grid, at, down_chain.block(received))
        down_sent, up_sent, grad_mixed = hold(down_line.give(1), up_sent, grad_mixed)
    one, sums_first = attend_backward(qkv, grad_mixed, doc_column, doc_row, 0)
    if grid.pairs:
        received, down_got, one, branch, grad_mixed = hold(
            up_chain.swap(up_sent), down_line.move(down_sent), one, branch, grad_mixed
        )
        up_sent, down_sent, one, branch = hold(
            up_chain.second(received), down_line.give(2, down_got), one, branch
        )
        of_qkv, of_out = halves(token_parts, one), halves(mixed_parts, branch)
        early = [jnp.concatenate([of_qkv[i], of_out[i]], axis=1) for i in range(2)]
        early_chain = Chain(grid, at, *early)
        early_sent, received, down_got = hold(
            early_chain.first(), up_chain.swap(up_sent), down_line.move(down_sent)
        )
        up_line = Line(grid, at, up_chain.block(received))
        up_sent, down_sent, early_sent, grad_mixed = hold(
            up_line.give(1), down_line.give(3, down_got), early_sent, grad_mixed
        )
    two, sums_second = attend_backward(qkv, grad_mixed, doc_column, doc_row, 1)
    if grid.pairs:
        received, up_got, down_got, two = hold(
            early_chain.swap(early_sent), up_line.move(up_sent), down_line.move(down_sent), two
        )
        early_sent, up_sent, two = hold(early_chain.second(received), up_line.give(2, up_got), two)
    sums_first, sums_second = sums_first[0], sums_second[0]
    totals = [
        jnp.concatenate([sums_first[:HALF], sums_second[:HALF]]),
        jnp.concatenate([sums_first[2 * HALF :], sums_second[2 * HALF :]]),
        sums_one[2],
        sums_one[0],
        sums_one[1],
        sums_up[0],
        sums_two[2],
        sums_two[0],
        sums_two[1],
    ]
    if grid.pairs:
        share_down = down_line.rest(down_got, grid.zs)
        packed = jnp.concatenate([v.reshape(grid.count, -1) for v in totals], axis=1)
        widths = [v.size // grid.count for v in totals]
        packed = jnp.pad(packed, ((0, 0), (0, rows * 128 - sum(widths)))).astype(jnp.bfloat16)
        packed = packed.reshape(grid.xs, CORES, -1, 128)
        ends = [take(packed, core_at, 1).reshape(-1, 128) for core_at in (1 - at["c"], at["c"])]
        of_qkv = halves(token_parts, two)
        late = [jnp.concatenate([of_qkv[i], ends[i]], axis=1) for i in range(2)]
        late_chain = Chain(grid, at, *late)
        late_sent, received, up_got = hold(
            late_chain.first(), early_chain.swap(early_sent), up_line.move(up_sent)
        )
        two, late_sent = hold(two, late_sent)
        tokens_grad = (
            grad_hidden
            + back_matmul(one, full_qkv[:, : 3 * HALF])
            + back_matmul(two, full_qkv[:, 3 * HALF :])
        ).astype(jnp.bfloat16)
        late_got, tokens_grad = hold(late_chain.swap(late_sent), tokens_grad)
        share_up = up_line.rest(up_got, 3)
        early_block = early_chain.block(received)
        late_sent = late_chain.second(late_got)
        late_block = late_chain.block(late_chain.swap(late_sent))
        line = Line(grid, at, jnp.concatenate([early_block, late_block], axis=2))
        block = line.rest(line.move(line.give(1)), 2)
        early, share_out = block[:, : 3 * HALF], block[:, 3 * HALF : 5 * HALF]
        late = block[:, 5 * HALF :]
        flat = late[:, 3 * HALF :].reshape(-1)
        shares, start = [], 0
        for width in widths:
            shares.append(flat[start : start + width])
            start += width
    else:
        share_down = plain_reduce(grid, active_parts, grad_low)
        share_up = plain_reduce(grid, first_parts, grad_up)
        share_out = plain_reduce(grid, mixed_parts, branch)
        early, late = plain_reduce(grid, token_parts, one), plain_reduce(grid, token_parts, two)
        shares = [lax.psum_scatter(v, AXES, scatter_dimension=0, tiled=True) for v in totals]
        tokens_grad = (
            grad_hidden
            + back_matmul(one, full_qkv[:, : 3 * HALF])
            + back_matmul(two, full_qkv[:, 3 * HALF :])
        ).astype(jnp.bfloat16)
    share_query, share_key, share_value = (
        jnp.concatenate([part[:, i : i + HALF] for part in (early, late)], axis=1)
        for i in range(0, 3 * HALF, HALF)
    )
    return (
        output,
        tokens_grad,
        share_query,
        shares[0],
        share_key,
        share_value,
        shares[1],
        share_out,
        *shares[2:5],
        share_up,
        shares[5],
        share_down,
        *shares[6:],
    )


def solution(mesh):
    rows, flat = P(AXES, None), P(AXES)
    in_specs = (rows,) * 3 + (flat, rows, rows, flat, rows, flat, flat, flat, rows, flat, rows)
    in_specs += (flat,) * 3 + (rows,)
    out_specs = (rows,) * 3 + (flat, rows, rows, flat, rows, flat, flat, flat, rows, flat, rows)
    out_specs += (flat,) * 3
    return jax.shard_map(
        functools.partial(per_device, Grid(mesh)),
        mesh=mesh,
        in_specs=in_specs,
        out_specs=out_specs,
        check_vma=False,
    )
```
